32 devices in a mesh: blk: 16 (over z, y, x), pts: 2 (over core).
Axes of the slice: x: 2, y: 2, z: 4, core: 2. Of those that a mesh axis runs over, the one named last changes fastest.
Arguments:
- snapshots: float32 [4096, 5, 256], P('blk', None, 'pts'), may hold values from -150 to 150
- weights: float32 [5, 256], P(None, 'pts'), may hold values from 0.3 to 3
- offsets: int32 [16], replicated, may hold values from 0 to 255, as said below
- freqs: int32 [64], replicated, may hold values from 1 to 127, as said below
Outputs:
- modes: float32 [64, 16, 2, 5, 256], P('blk', None, None, None, 'pts')
- spectrum: float32 [64, 16], P('blk')
The draws below stay inside these ranges and needn't reach their ends.
Inputs may be any that keep to these rules, and one draw needn't show every extreme that they name: Block b covers snapshots b * 256 + offsets[b] onward, 256 of them; the last block's offset is 0 and some other block's is 255. `freqs`: distinct and increasing; 1 and 127 are among them.
All inputs are finite; a program needn't handle non-finite values.
Results may differ from the reference program's by a relative error of at most 0.008.
Values sent between devices are 32-bit elements; how exact they have to be, the bound alone decides.
A program may use at most 64 MiB of HBM per device.

```python
import math
import jax
import jax.numpy as jnp
from jax import lax

NFFT = 256
NF = 64
VARS = 5
SWEEPS = 2
NB = 16
NT = 4096
NP = 256


def draw_snapshots(key, part):
    key_noise, key_amp, key_shape, key_scale = jax.random.split(key, 4)
    width = VARS * NP
    times = jnp.arange(NT, dtype=jnp.float32) / NT
    envelope = 1.0 + 2.0 * times
    amplitude = jax.random.normal(key_amp, (NT, 4), jnp.float32)
    pattern = jax.random.normal(key_shape, (4, width), jnp.float32)
    point_scale = jnp.exp(jax.random.uniform(key_scale, (1, width), jnp.float32, 0.0, 2.3))
    white = jnp.clip(jax.random.normal(key_noise, (NT + 1, width), jnp.float32), -4.0, 4.0)
    level = 0.7
    colored = level * white[1:] + (white[1:] - white[:-1])
    field = colored * point_scale
    field = field + amplitude[:, 0:1] * pattern[0:1]
    field = field + amplitude[:, 1:2] * pattern[1:2]
    field = field + amplitude[:, 2:3] * pattern[2:3]
    field = field + amplitude[:, 3:4] * pattern[3:4]
    field = jnp.clip(envelope[:, None] * field, -150.0, 150.0)
    return field.reshape(NT, VARS, NP)


def draw_offsets(key, part):
    key_base, key_pick = jax.random.split(key, 2)
    drawn = jax.random.randint(key_base, (NB,), 0, NFFT, dtype=jnp.int32)
    chosen = jax.random.randint(key_pick, (), 0, NB - 1, dtype=jnp.int32)
    position = jnp.arange(NB, dtype=jnp.int32)
    drawn = jnp.where(position == chosen, NFFT - 1, drawn)
    return jnp.where(position == NB - 1, 0, drawn).astype(jnp.int32)


def draw_freqs(key, part):
    interior = 2 + jax.random.permutation(key, NFFT // 2 - 3)[:NF - 2].astype(jnp.int32)
    picked = jnp.concatenate([jnp.array([1, NFFT // 2 - 1], dtype=jnp.int32), interior])
    return jnp.sort(picked).astype(jnp.int32)


def steps_of(stream_key, dims, cuts, low, top_value):
    def one(dim, shards_of):
        steps = jax.random.uniform(jax.random.fold_in(jax.random.fold_in(stream_key, 6), dim), (shards_of,), jnp.float32, low / len(cuts), top_value / len(cuts))
        return jnp.repeat(jnp.exp(steps), dims[dim] // shards_of).reshape((-1,) + (1,) * (len(dims) - dim - 1))

    factor_of = one(*cuts[0])
    for cut in cuts[1:]:
        factor_of = factor_of * one(*cut)
    return factor_of


def setup_inputs(seed: int = 0) -> dict:
    streams_of = jax.random.split(jax.random.key(seed), 5)
    snapshots = draw_snapshots(jax.random.fold_in(streams_of[4], 71), 0)
    weights = jnp.clip(jnp.exp(math.log(3.0) - 2.3025851 * jax.random.uniform(streams_of[1], (VARS, NP), jnp.float32) ** steps_of(streams_of[1], (VARS, NP), ((1, 2),), -0.2, 0.2)), 0.3, 3.0)
    offsets = draw_offsets(jax.random.fold_in(streams_of[4], 71), 0)
    freqs = draw_freqs(jax.random.fold_in(streams_of[4], 71), 0)
    return dict(snapshots=snapshots, weights=weights, offsets=offsets, freqs=freqs)


HIGH = lax.Precision.HIGHEST
DAMPING = 0.01

def spectral_table(freqs, lags, valid, nfft):
    phase_index = jnp.mod(freqs[:, None] * lags[None, :], nfft)
    angle = 2.0 * math.pi / nfft * phase_index.astype(jnp.float32)
    hann = 0.5 - 0.5 * jnp.cos(2.0 * math.pi / nfft * lags.astype(jnp.float32))
    factor = jnp.where(valid, hann, 0.0) / math.sqrt(nfft)
    table = jnp.stack([factor[None, :] * jnp.cos(angle), -factor[None, :] * jnp.sin(angle)], axis=1)
    return table.reshape(2 * freqs.shape[0], nfft)

def rotate_round(carry, round_index):
    real_a, imag_a, real_v, imag_v = carry
    count = real_a.shape[-1]
    index = jnp.arange(count, dtype=jnp.int32)
    mirror = jnp.mod(2 * round_index - index, count - 1).astype(jnp.int32)
    partner = jnp.where(index == count - 1, round_index, jnp.where(index == round_index, count - 1, mirror)).astype(jnp.int32)
    parity = jnp.where(index < partner, 1.0, -1.0).astype(jnp.float32)
    diagonal = jnp.diagonal(real_a, axis1=-2, axis2=-1)
    diag_pair = jnp.take(diagonal, partner, axis=-1)
    columns = jnp.broadcast_to(partner[:, None], real_a.shape[:-1] + (1,))
    pair_real = jnp.take_along_axis(real_a, columns, axis=-1)[..., 0]
    pair_imag = jnp.take_along_axis(imag_a, columns, axis=-1)[..., 0]
    delta = parity * (diag_pair - diagonal)
    size_sq = pair_real * pair_real + pair_imag * pair_imag
    radius = jnp.sqrt(delta * delta + 4.0 * size_sq)
    upper = radius + delta + DAMPING * (diagonal + diag_pair)
    length = jnp.sqrt(upper * upper + 4.0 * size_sq)
    cosine = upper / length
    off_real = 2.0 * parity * pair_real / length
    off_imag = 2.0 * parity * pair_imag / length
    moved_real = jnp.take(off_real, partner, axis=-1)
    moved_imag = jnp.take(off_imag, partner, axis=-1)

    def right_apply(left_real, left_imag):
        swap_real = jnp.take(left_real, partner, axis=-1)
        swap_imag = jnp.take(left_imag, partner, axis=-1)
        coef_c = cosine[..., None, :]
        coef_r = moved_real[..., None, :]
        coef_i = moved_imag[..., None, :]
        return (left_real * coef_c + swap_real * coef_r - swap_imag * coef_i, left_imag * coef_c + swap_real * coef_i + swap_imag * coef_r)

    def left_apply(right_real, right_imag):
        swap_real = jnp.take(right_real, partner, axis=-2)
        swap_imag = jnp.take(right_imag, partner, axis=-2)
        coef_c = cosine[..., :, None]
        coef_r = moved_real[..., :, None]
        coef_i = moved_imag[..., :, None]
        return (right_real * coef_c + swap_real * coef_r + swap_imag * coef_i, right_imag * coef_c + swap_imag * coef_r - swap_real * coef_i)
    half_real, half_imag = right_apply(real_a, imag_a)
    new_real, new_imag = left_apply(half_real, half_imag)
    vec_real, vec_imag = right_apply(real_v, imag_v)
    return (new_real, new_imag, vec_real, vec_imag)

def jacobi_solve(gram_real, gram_imag):
    count = gram_real.shape[-1]
    identity = jnp.broadcast_to(jnp.eye(count, dtype=gram_real.dtype), gram_real.shape)
    state = (gram_real, gram_imag, identity, jnp.zeros_like(gram_real))

    def advance(counter, carry):
        return rotate_round(carry, jnp.mod(counter, count - 1).astype(jnp.int32))
    return lax.fori_loop(0, SWEEPS * (count - 1), advance, state)

def mode_factors(real_a, real_v, imag_v, nblocks):
    eigen = jnp.diagonal(real_a, axis1=-2, axis2=-1)
    sum_real = lax.optimization_barrier(jnp.sum(real_v, axis=-2))
    sum_imag = lax.optimization_barrier(jnp.sum(imag_v, axis=-2))
    magnitude = jnp.sqrt(sum_real * sum_real + sum_imag * sum_imag)
    scaling = 1.0 / (jnp.maximum(magnitude, 1.0) * jnp.sqrt(nblocks * (eigen + 1e-06)))
    phase_real = (sum_real * scaling)[..., None, :]
    phase_imag = (-sum_imag * scaling)[..., None, :]
    coef_real = real_v * phase_real - imag_v * phase_imag
    coef_imag = real_v * phase_imag + imag_v * phase_real
    return (eigen, coef_real, coef_imag)

def reference(snapshots, weights, offsets, freqs):
    ntime, nvars, npoints = snapshots.shape
    nfreq = freqs.shape[0]
    width = nvars * npoints
    lags = jnp.arange(NFFT, dtype=jnp.int32)
    table = spectral_table(freqs, lags, lags >= 0, NFFT)

    def block_spectra(block_index):
        start = (block_index * NFFT + offsets[block_index]).astype(jnp.int32)
        segment = lax.dynamic_slice(snapshots, (start, jnp.int32(0), jnp.int32(0)), (NFFT, nvars, npoints))
        return jnp.dot(table, segment.reshape(NFFT, width), precision=HIGH).reshape(nfreq, 2, width)
    spectra = lax.map(block_spectra, jnp.arange(NB, dtype=jnp.int32))
    flat_weights = weights.reshape(1, width)
    gram_scale = 1.0 / (NB * nvars * npoints)

    def gram_of(freq_index):
        piece = lax.dynamic_index_in_dim(spectra, freq_index, 1, keepdims=False)
        part_real = piece[:, 0]
        part_imag = piece[:, 1]
        weighted_real = part_real * flat_weights
        weighted_imag = part_imag * flat_weights
        gram_real = (jnp.dot(weighted_real, part_real.T, precision=HIGH) + jnp.dot(weighted_imag, part_imag.T, precision=HIGH)) * gram_scale
        gram_imag = (jnp.dot(weighted_real, part_imag.T, precision=HIGH) - jnp.dot(weighted_imag, part_real.T, precision=HIGH)) * gram_scale
        return (gram_real, gram_imag)
    gram_real, gram_imag = lax.map(gram_of, jnp.arange(nfreq, dtype=jnp.int32))
    real_a, imag_a, real_v, imag_v = jacobi_solve(gram_real, gram_imag)
    eigen, coef_real, coef_imag = mode_factors(real_a, real_v, imag_v, NB)

    def modes_of(freq_index):
        piece = lax.dynamic_index_in_dim(spectra, freq_index, 1, keepdims=False)
        part_real = piece[:, 0]
        part_imag = piece[:, 1]
        crl = lax.dynamic_index_in_dim(coef_real, freq_index, 0, keepdims=False)
        cim = lax.dynamic_index_in_dim(coef_imag, freq_index, 0, keepdims=False)
        mode_real = jnp.dot(crl.T, part_real, precision=HIGH) - jnp.dot(cim.T, part_imag, precision=HIGH)
        mode_imag = jnp.dot(cim.T, part_real, precision=HIGH) + jnp.dot(crl.T, part_imag, precision=HIGH)
        return jnp.stack([mode_real, mode_imag], axis=1).reshape(NB, 2, nvars, npoints)
    modes = lax.map(modes_of, jnp.arange(nfreq, dtype=jnp.int32))
    total = jnp.sum(eigen)
    spectrum = nfreq * NB * eigen / total
    return (modes, spectrum)
```

```python
import functools
import math

import jax
import jax.numpy as jnp
from jax import lax
from jax.experimental import pallas as pl
from jax.experimental.pallas import tpu as pltpu
from jax.sharding import PartitionSpec as P

SWEEPS = 2


HIGH = lax.Precision.HIGHEST
DAMPING = 0.01


def passed_along(block, axis, distance):
    devices = range(lax.axis_size(axis))
    route = [(i - distance, i) for i in devices if i - distance in devices]
    return lax.ppermute(block, axis, route)


def spectral_table(freqs, lags, valid, nfft):
    phase_index = jnp.mod(freqs[:, None] * lags[None, :], nfft)
    angle = 2.0 * math.pi / nfft * phase_index.astype(jnp.float32)
    hann = 0.5 - 0.5 * jnp.cos(2.0 * math.pi / nfft * lags.astype(jnp.float32))
    factor = jnp.where(valid, hann, 0.0) / math.sqrt(nfft)
    table = jnp.stack([factor[None, :] * jnp.cos(angle), -factor[None, :] * jnp.sin(angle)], axis=1)
    return table.reshape(2 * freqs.shape[0], nfft)


def half_turned(row, half):
    return pltpu.roll(row, half, 1)


def lane_gather(block, index):
    rows = max(block.shape[0], 8)
    wide = jnp.broadcast_to(block, (rows, block.shape[1]))
    index = jnp.broadcast_to(index, wide.shape)
    return jnp.take_along_axis(wide, index, axis=1, mode="promise_in_bounds")[: block.shape[0]]


def jacobi_on_lanes(gram, count, groups):
    half = groups * count
    lanes = 2 * half
    lane = lax.broadcasted_iota(jnp.int32, (1, lanes), 1)
    column = lax.rem(lane, count)
    first = lane - column
    in_real = lane < half
    sign = jnp.where(in_real, 1.0, -1.0).astype(jnp.float32)
    row = lax.broadcasted_iota(jnp.int32, (count, lanes), 0)
    on_diagonal = row == column
    eye = jnp.where(on_diagonal & in_real, 1.0, 0.0).astype(jnp.float32)
    real_diag = jnp.sum(gram * eye, axis=0, keepdims=True)
    diag = real_diag + half_turned(real_diag, half)

    def advance(counter, carry):
        vec, prod, diag = carry
        turn = lax.rem(counter, count - 1)
        mirror = 2 * turn - column
        mirror = jnp.where(mirror < 0, mirror + (count - 1), mirror)
        mirror = jnp.where(mirror >= count - 1, mirror - (count - 1), mirror)
        partner = jnp.where(column == count - 1, turn, jnp.where(column == turn, count - 1, mirror))
        parity = jnp.where(column < partner, 1.0, -1.0).astype(jnp.float32)
        same = first + partner
        other = jnp.where(same < half, same + half, same - half)
        prod_same = lane_gather(prod, same)
        prod_other = lane_gather(prod, other)
        vec_same = lane_gather(vec, same)
        vec_other = lane_gather(vec, other)
        diag_pair = lane_gather(diag, same)
        pair_real = jnp.sum(vec * prod_same, axis=0, keepdims=True)
        pair_real = pair_real + half_turned(pair_real, half)
        pair_imag = sign * jnp.sum(vec * prod_other, axis=0, keepdims=True)
        pair_imag = pair_imag + half_turned(pair_imag, half)
        delta = parity * (diag_pair - diag)
        size4 = 4.0 * (pair_real * pair_real + pair_imag * pair_imag)
        radius = jnp.sqrt(delta * delta + size4)
        upper = radius + delta + DAMPING * (diag + diag_pair)
        inverse = lax.rsqrt(upper * upper + size4)
        cosine = upper * inverse
        scale = 2.0 * parity * inverse
        coef_r = -scale * pair_real
        coef_i = -sign * scale * pair_imag
        sine_sq = size4 * inverse * inverse
        diag = cosine * cosine * diag + sine_sq * diag_pair - parity * cosine * size4 * inverse
        vec = vec * cosine + vec_same * coef_r + vec_other * coef_i
        prod = prod * cosine + prod_same * coef_r + prod_other * coef_i
        return vec, prod, diag

    vec, _, eigen = lax.fori_loop(0, SWEEPS * (count - 1), advance, (eye, gram, diag))
    sums = jnp.sum(vec, axis=0, keepdims=True)
    turned = half_turned(sums, half)
    magnitude = jnp.sqrt(sums * sums + turned * turned)
    scaling = 1.0 / (jnp.maximum(magnitude, 1.0) * jnp.sqrt(count * (eigen + 1e-06)))
    phase_real = jnp.where(in_real, sums, turned) * scaling
    phase_imag = -jnp.where(in_real, turned, sums) * scaling
    coef = vec * phase_real - half_turned(vec, half) * (sign * phase_imag)
    return coef, eigen


def jacobi_kernel(count, groups, gram_ref, coef_ref, eigen_ref):
    coef, eigen = jacobi_on_lanes(gram_ref[...], count, groups)
    coef_ref[...] = coef
    eigen_ref[...] = jnp.broadcast_to(eigen, eigen_ref.shape)


def jacobi_call(gram_real, gram_imag):
    groups, count, _ = gram_real.shape
    half = groups * count
    gram = jnp.stack([gram_real, gram_imag]).transpose(2, 0, 1, 3).reshape(count, 2 * half)
    coef, eigen = pl.pallas_call(
        functools.partial(jacobi_kernel, count, groups),
        out_shape=(
            jax.ShapeDtypeStruct((count, 2 * half), jnp.float32),
            jax.ShapeDtypeStruct((8, 2 * half), jnp.float32),
        ),
        in_specs=[pl.BlockSpec(memory_space=pltpu.VMEM)],
        out_specs=(pl.BlockSpec(memory_space=pltpu.VMEM), pl.BlockSpec(memory_space=pltpu.VMEM)),
    )(gram)
    coef = coef.reshape(count, 2, groups, count)
    return eigen[0, :half].reshape(groups, count), coef[:, 0].transpose(1, 0, 2), coef[:, 1].transpose(1, 0, 2)


def body(snapshots, weights, offsets, freqs):
    nfft, nvars, npts = snapshots.shape
    nfreq = freqs.shape[0]
    nblocks = lax.axis_size("blk")
    total_pts = npts * lax.axis_size("pts")
    width = nvars * npts
    block = lax.axis_index("blk")
    lags = jnp.arange(nfft, dtype=jnp.int32)
    flat = snapshots.reshape(nfft, width)
    own_off = offsets[block]
    own_table = spectral_table(freqs, lags - own_off, lags >= own_off, nfft)
    spectra = jnp.dot(own_table, flat, precision=HIGH)
    following = passed_along(flat, "blk", -1)
    tail_table = spectral_table(freqs, lags + nfft - own_off, lags < own_off, nfft)
    spectra = spectra + jnp.dot(tail_table, following, precision=HIGH)
    spectra = spectra.reshape(nfreq, 2, nvars, npts)
    gram_scale = 1.0 / (nblocks * nvars * total_pts)
    grouped = lax.all_to_all(spectra[:, None], "blk", split_axis=0, concat_axis=1, tiled=True)
    local_freqs = grouped.shape[0]
    part_real = grouped[:, :, 0].reshape(local_freqs, nblocks, width)
    part_imag = grouped[:, :, 1].reshape(local_freqs, nblocks, width)
    flat_weights = weights.reshape(1, 1, width)
    weighted_real = part_real * flat_weights
    weighted_imag = part_imag * flat_weights
    gram_real = (
        jnp.einsum("fbx,fcx->fbc", weighted_real, part_real, precision=HIGH)
        + jnp.einsum("fbx,fcx->fbc", weighted_imag, part_imag, precision=HIGH)
    ) * gram_scale
    gram_imag = (
        jnp.einsum("fbx,fcx->fbc", weighted_real, part_imag, precision=HIGH)
        - jnp.einsum("fbx,fcx->fbc", weighted_imag, part_real, precision=HIGH)
    ) * gram_scale
    gram_real, gram_imag = lax.psum((gram_real, gram_imag), "pts")
    total = lax.psum(jnp.sum(jnp.diagonal(gram_real, axis1=-2, axis2=-1)), "blk")
    eigen, coef_real, coef_imag = jacobi_call(gram_real, gram_imag)
    mode_real = jnp.einsum("fbx,fbm->fmx", part_real, coef_real, precision=HIGH) - jnp.einsum(
        "fbx,fbm->fmx", part_imag, coef_imag, precision=HIGH
    )
    mode_imag = jnp.einsum("fbx,fbm->fmx", part_real, coef_imag, precision=HIGH) + jnp.einsum(
        "fbx,fbm->fmx", part_imag, coef_real, precision=HIGH
    )
    modes = jnp.stack([mode_real, mode_imag], axis=2).reshape(local_freqs, nblocks, 2, nvars, npts)
    spectrum = nfreq * nblocks * eigen / total
    return (modes, spectrum)


def solution(mesh):
    return jax.shard_map(
        body,
        mesh=mesh,
        in_specs=(P("blk", None, "pts"), P(None, "pts"), P(), P()),
        out_specs=(P("blk", None, None, None, "pts"), P("blk", None)),
        check_vma=False,
    )
```

```python
import functools
import math

import jax
import jax.numpy as jnp
from jax import lax
from jax.experimental import pallas as pl
from jax.experimental.pallas import tpu as pltpu
from jax.sharding import PartitionSpec as P

SWEEPS = 2


HIGH = lax.Precision.HIGHEST
DAMPING = 0.01
MESH = pl.DeviceIdType.MESH


def half_turned(row, half):
    return pltpu.roll(row, half, 1)


def lane_gather(block, index):
    rows = max(block.shape[0], 8)
    wide = jnp.broadcast_to(block, (rows, block.shape[1]))
    index = jnp.broadcast_to(index, wide.shape)
    return jnp.take_along_axis(wide, index, axis=1, mode="promise_in_bounds")[: block.shape[0]]


def jacobi_on_lanes(gram, count, groups):
    half = groups * count
    lanes = 2 * half
    lane = lax.broadcasted_iota(jnp.int32, (1, lanes), 1)
    column = lax.rem(lane, count)
    first = lane - column
    in_real = lane < half
    sign = jnp.where(in_real, 1.0, -1.0).astype(jnp.float32)
    row = lax.broadcasted_iota(jnp.int32, (count, lanes), 0)
    on_diagonal = row == column
    eye = jnp.where(on_diagonal & in_real, 1.0, 0.0).astype(jnp.float32)
    real_diag = jnp.sum(gram * eye, axis=0, keepdims=True)
    diag = real_diag + half_turned(real_diag, half)

    def advance(counter, carry):
        vec, prod, diag = carry
        turn = lax.rem(counter, count - 1)
        mirror = 2 * turn - column
        mirror = jnp.where(mirror < 0, mirror + (count - 1), mirror)
        mirror = jnp.where(mirror >= count - 1, mirror - (count - 1), mirror)
        partner = jnp.where(column == count - 1, turn, jnp.where(column == turn, count - 1, mirror))
        parity = jnp.where(column < partner, 1.0, -1.0).astype(jnp.float32)
        same = first + partner
        other = jnp.where(same < half, same + half, same - half)
        prod_same = lane_gather(prod, same)
        prod_other = lane_gather(prod, other)
        vec_same = lane_gather(vec, same)
        vec_other = lane_gather(vec, other)
        diag_pair = lane_gather(diag, same)
        pair_real = jnp.sum(vec * prod_same, axis=0, keepdims=True)
        pair_real = pair_real + half_turned(pair_real, half)
        pair_imag = sign * jnp.sum(vec * prod_other, axis=0, keepdims=True)
        pair_imag = pair_imag + half_turned(pair_imag, half)
        delta = parity * (diag_pair - diag)
        size4 = 4.0 * (pair_real * pair_real + pair_imag * pair_imag)
        radius = jnp.sqrt(delta * delta + size4)
        upper = radius + delta + DAMPING * (diag + diag_pair)
        inverse = lax.rsqrt(upper * upper + size4)
        cosine = upper * inverse
        scale = 2.0 * parity * inverse
        coef_r = -scale * pair_real
        coef_i = -sign * scale * pair_imag
        sine_sq = size4 * inverse * inverse
        diag = cosine * cosine * diag + sine_sq * diag_pair - parity * cosine * size4 * inverse
        vec = vec * cosine + vec_same * coef_r + vec_other * coef_i
        prod = prod * cosine + prod_same * coef_r + prod_other * coef_i
        return vec, prod, diag

    vec, _, eigen = lax.fori_loop(0, SWEEPS * (count - 1), advance, (eye, gram, diag))
    sums = jnp.sum(vec, axis=0, keepdims=True)
    turned = half_turned(sums, half)
    magnitude = jnp.sqrt(sums * sums + turned * turned)
    scaling = 1.0 / (jnp.maximum(magnitude, 1.0) * jnp.sqrt(count * (eigen + 1e-06)))
    phase_real = jnp.where(in_real, sums, turned) * scaling
    phase_imag = -jnp.where(in_real, turned, sums) * scaling
    coef = vec * phase_real - half_turned(vec, half) * (sign * phase_imag)
    return coef, eigen


def signed_wave(base, index):
    lanes = base.shape[1]
    value = lane_gather(base, jnp.bitwise_and(index, lanes - 1))
    return jnp.where(jnp.bitwise_and(index, lanes) == 0, value, -value)


def write_table(table_ref, offsets_ref, freqs_ref, me, groups):
    rows, nfft = table_ref.shape
    half = nfft // 2
    lane = lax.broadcasted_iota(jnp.int32, (8, half), 1)
    sub = lax.broadcasted_iota(jnp.int32, (8, half), 0)
    base = jnp.cos(2.0 * math.pi / nfft * lane.astype(jnp.float32))
    own = offsets_ref[me]
    before = jnp.where(me > 0, offsets_ref[jnp.maximum(me - 1, 0)], 0)
    quarter = jnp.where(lax.rem(sub, 2) == 1, nfft // 4, 0)
    windows = {}
    for tile in range(rows // 8):
        tile_rows = range(8 * tile, 8 * tile + 8)
        pieces = tuple(r % (4 * groups) // (2 * groups) for r in tile_rows)
        freq = [r // (4 * groups) * groups + r % (2 * groups) // 2 for r in tile_rows]
        freq_rows = jnp.full((8, half), freqs_ref[freq[0]], jnp.int32)
        for s in range(2, 8, 2):
            freq_rows = jnp.where(sub >= s, freqs_ref[freq[s]], freq_rows)
        if pieces not in windows:
            tail = jnp.zeros((8, half), jnp.bool_)
            for s in range(8):
                if pieces[s]:
                    tail = tail | (sub == s)
            start = jnp.where(tail, before, own)
            window = []
            for h in range(2):
                lag = lane + h * half - start
                hann = 0.5 - 0.5 * signed_wave(base, lag)
                valid = (tail & (lag < 0)) | (jnp.logical_not(tail) & (lag >= 0))
                window.append((lag, jnp.where(valid, hann, 0.0) / math.sqrt(nfft)))
            windows[pieces] = window
        for h in range(2):
            lag, factor = windows[pieces][h]
            wave = signed_wave(base, freq_rows * lag + quarter)
            table_ref[8 * tile : 8 * tile + 8, h * half : (h + 1) * half] = factor * wave


def pipeline_kernel(
    nblocks, npart, groups, scale, energy,
    snaps_ref, weights_ref, offsets_ref, freqs_ref, modes_ref, spectrum_ref,
    table, stage, recv, spectra, gram_part, total_part,
    send_sem, recv_sem, gram_send, gram_recv, total_send, total_recv,
):
    me = lax.axis_index("blk")
    side = lax.axis_index("pts")
    nfft, nvars, npts = snaps_ref.shape
    rows = 2 * groups * nblocks
    half = rows // 2
    piece = 2 * groups

    def block_peer(k):
        return lax.rem(me + k, nblocks)

    def side_peer(k):
        return lax.rem(side + k, npart)

    barrier = pltpu.get_barrier_semaphore()
    for k in range(1, nblocks):
        pl.semaphore_signal(barrier, inc=1, device_id={"blk": block_peer(k)}, device_id_type=MESH)
    for k in range(1, npart):
        pl.semaphore_signal(barrier, inc=1, device_id={"pts": side_peer(k)}, device_id_type=MESH)

    write_table(table, offsets_ref, freqs_ref, me, groups)
    for v in range(nvars):
        part = jnp.dot(table[...], snaps_ref[:, v, :], precision=HIGH, preferred_element_type=jnp.float32)
        for g in range(nblocks):
            stage[g, :, v * npts : (v + 1) * npts] = part[2 * piece * g : 2 * piece * (g + 1)]

    pl.semaphore_wait(barrier, nblocks - 1 + npart - 1)

    def spectra_copy(k, slot):
        peer = block_peer(k)
        return pltpu.make_async_remote_copy(
            src_ref=stage.at[peer], dst_ref=recv.at[slot], send_sem=send_sem.at[k],
            recv_sem=recv_sem.at[slot], device_id={"blk": peer}, device_id_type=MESH,
        )

    for k in range(1, nblocks):
        spectra_copy(k, me).start()
    recv[me] = stage[me]
    recv[nblocks] = jnp.zeros(recv.shape[1:], jnp.float32)
    for k in range(1, nblocks):
        spectra_copy(k, block_peer(k)).wait_recv()

    for ri in range(2):
        for f in range(groups):
            at = (ri * groups + f) * nblocks
            own = recv[0:nblocks, 2 * f + ri, :]
            tail = recv[1 : nblocks + 1, piece + 2 * f + ri, :]
            spectra[at : at + nblocks, :] = own + tail

    gram_all = jnp.zeros((rows, rows), jnp.float32)
    for v in range(nvars):
        part = spectra[:, v * npts : (v + 1) * npts]
        gram_all = gram_all + lax.dot_general(
            part * weights_ref[v : v + 1, :], part, (((1,), (1,)), ((), ())),
            precision=HIGH, preferred_element_type=jnp.float32,
        )
    lane = lax.broadcasted_iota(jnp.int32, (1, rows), 1)
    sign = jnp.where(lane < half, 1.0, -1.0).astype(jnp.float32)
    group_of = lax.rem(lane, half) // nblocks
    gram = jnp.zeros((nblocks, rows), jnp.float32)
    for f in range(groups):
        upper = gram_all[f * nblocks : (f + 1) * nblocks]
        lower = gram_all[half + f * nblocks : half + (f + 1) * nblocks]
        gram = jnp.where(group_of == f, upper + sign * pltpu.roll(lower, half, 1), gram)
    gram_part[side] = gram * scale

    def gram_copy(k, slot):
        peer = side_peer(k)
        return pltpu.make_async_remote_copy(
            src_ref=gram_part.at[side], dst_ref=gram_part.at[slot], send_sem=gram_send.at[k],
            recv_sem=gram_recv.at[slot], device_id={"pts": peer}, device_id_type=MESH,
        )

    for k in range(1, npart):
        gram_copy(k, side).start()
    for k in range(1, npart):
        gram_copy(k, side_peer(k)).wait_recv()
    gram = gram_part[0]
    for k in range(1, npart):
        gram = gram + gram_part[k]

    row = lax.broadcasted_iota(jnp.int32, (nblocks, rows), 0)
    trace = jnp.where((row == lax.rem(lane, nblocks)) & (lane < half), gram, 0.0)
    trace = jnp.sum(jnp.sum(trace, axis=0, keepdims=True), axis=1, keepdims=True)
    total_part[me] = jnp.broadcast_to(trace, total_part.shape[1:])

    def total_copy(k, slot):
        peer = block_peer(k)
        return pltpu.make_async_remote_copy(
            src_ref=total_part.at[me], dst_ref=total_part.at[slot], send_sem=total_send.at[k],
            recv_sem=total_recv.at[slot], device_id={"blk": peer}, device_id_type=MESH,
        )

    for k in range(1, nblocks):
        total_copy(k, me).start()

    coef, eigen = jacobi_on_lanes(gram, nblocks, groups)

    turned = -sign * half_turned(coef, half)
    pieces = [jnp.where(group_of == f, block, 0.0) for block in (coef, turned) for f in range(groups)]
    mixing = jnp.concatenate(pieces, axis=0).T
    modes_ref[...] = jnp.dot(mixing, spectra[...], precision=HIGH, preferred_element_type=jnp.float32)

    for k in range(1, nblocks):
        total_copy(k, block_peer(k)).wait_recv()
    total = jnp.sum(total_part[...], axis=0)
    spectrum_ref[...] = energy * eigen / total
    for k in range(1, nblocks):
        spectra_copy(k, me).wait_send()
        total_copy(k, me).wait_send()
    for k in range(1, npart):
        gram_copy(k, side).wait_send()


def body(snapshots, weights, offsets, freqs):
    nfft, nvars, npts = snapshots.shape
    nfreq = freqs.shape[0]
    nblocks = lax.axis_size("blk")
    npart = lax.axis_size("pts")
    groups = nfreq // nblocks
    width = nvars * npts
    rows = 2 * nfreq
    scale = 1.0 / (nblocks * nvars * npts * npart)
    dma = pltpu.SemaphoreType.DMA
    vmem = pl.BlockSpec(memory_space=pltpu.VMEM)
    smem = pl.BlockSpec(memory_space=pltpu.SMEM)
    modes, spectrum = pl.pallas_call(
        functools.partial(pipeline_kernel, nblocks, npart, groups, scale, float(nfreq * nblocks)),
        out_shape=(
            jax.ShapeDtypeStruct((rows, width), jnp.float32),
            jax.ShapeDtypeStruct((8, rows), jnp.float32),
        ),
        in_specs=[vmem, vmem, smem, smem],
        out_specs=(vmem, vmem),
        scratch_shapes=[
            pltpu.VMEM((2 * rows, nfft), jnp.float32),
            pltpu.VMEM((nblocks, 4 * groups, width), jnp.float32),
            pltpu.VMEM((nblocks + 1, 4 * groups, width), jnp.float32),
            pltpu.VMEM((rows, width), jnp.float32),
            pltpu.VMEM((npart, nblocks, rows), jnp.float32),
            pltpu.VMEM((nblocks, 8, rows), jnp.float32),
            dma((nblocks,)), dma((nblocks,)),
            dma((npart,)), dma((npart,)),
            dma((nblocks,)), dma((nblocks,)),
        ],
        compiler_params=pltpu.CompilerParams(
            collective_id=0, has_side_effects=True, vmem_limit_bytes=32 * 1024 * 1024
        ),
    )(snapshots, weights, offsets, freqs)
    modes = modes.reshape(2, groups, nblocks, nvars, npts).transpose(1, 2, 0, 3, 4)
    return modes, spectrum[0, :nfreq].reshape(groups, nblocks)


def solution(mesh):
    return jax.shard_map(
        body,
        mesh=mesh,
        in_specs=(P("blk", None, "pts"), P(None, "pts"), P(), P()),
        out_specs=(P("blk", None, None, None, "pts"), P("blk", None)),
        check_vma=False,
    )
```

```python
import functools
import math

import jax
import jax.numpy as jnp
from jax import lax
from jax.experimental import pallas as pl
from jax.experimental.pallas import tpu as pltpu
from jax.sharding import PartitionSpec as P

SWEEPS = 2


HIGH = lax.Precision.HIGHEST
DAMPING = 0.01
CHUNKS = 2
MESH = pl.DeviceIdType.MESH


def half_turned(row, half):
    return pltpu.roll(row, half, 1)


def lane_gather(block, index):
    rows = max(block.shape[0], 8)
    wide = jnp.broadcast_to(block, (rows, block.shape[1]))
    index = index if index.shape == wide.shape else jnp.broadcast_to(index[:1], wide.shape)
    return jnp.take_along_axis(wide, index, axis=1, mode="promise_in_bounds")[: block.shape[0]]


def jacobi_on_lanes(gram, count, groups):
    half = groups * count
    lanes = 2 * half
    lane = lax.broadcasted_iota(jnp.int32, (8, lanes), 1)
    column = lax.rem(lane, count)
    first = lane - column
    in_real = lane[:1] < half
    row = lax.broadcasted_iota(jnp.int32, (count, lanes), 0)
    eye = jnp.where(row == column[:1], 1.0, 0.0).astype(jnp.float32)
    turned = half_turned(gram, half)
    prod_r = jnp.where(in_real, gram, turned)
    prod_i = jnp.where(in_real, turned, gram)
    diag = jnp.sum(prod_r * eye, axis=0, keepdims=True)

    def partner_of(turn):
        mirror = 2 * turn - column
        mirror = jnp.where(mirror < 0, mirror + (count - 1), mirror)
        mirror = jnp.where(mirror >= count - 1, mirror - (count - 1), mirror)
        return jnp.where(column == count - 1, turn, jnp.where(column == turn, count - 1, mirror))

    def advance(counter, carry):
        vec_r, vec_i, prod_r, prod_i, diag, partner = carry
        following = partner_of(lax.rem(counter + 1, count - 1))
        parity = jnp.where(column < partner, 1.0, -1.0).astype(jnp.float32)[:1]
        same = first + partner
        prod_sr = lane_gather(prod_r, same)
        prod_si = lane_gather(prod_i, same)
        diag_pair = lane_gather(diag, same)
        vec_sr = lane_gather(vec_r, same)
        vec_si = lane_gather(vec_i, same)
        pair_real = jnp.sum(vec_r * prod_sr + vec_i * prod_si, axis=0, keepdims=True)
        pair_imag = jnp.sum(vec_r * prod_si - vec_i * prod_sr, axis=0, keepdims=True)
        delta = parity * (diag_pair - diag)
        size4 = 4.0 * (pair_real * pair_real + pair_imag * pair_imag)
        radius = jnp.sqrt(delta * delta + size4)
        upper = radius + (delta + DAMPING * (diag + diag_pair))
        inverse = lax.rsqrt(upper * upper + size4)
        cosine = upper * inverse
        scale = 2.0 * parity * inverse
        coef_r = -scale * pair_real
        coef_i = scale * pair_imag
        sine_sq = size4 * inverse * inverse
        diag = cosine * cosine * diag + sine_sq * diag_pair - parity * cosine * size4 * inverse

        def turn_pair(real, imag, swap_real, swap_imag):
            return (
                real * cosine + (swap_real * coef_r - swap_imag * coef_i),
                imag * cosine + (swap_real * coef_i + swap_imag * coef_r),
            )

        prod_r, prod_i = turn_pair(prod_r, prod_i, prod_sr, prod_si)
        vec_r, vec_i = turn_pair(vec_r, vec_i, vec_sr, vec_si)
        return vec_r, vec_i, prod_r, prod_i, diag, following

    state = (eye, jnp.zeros_like(eye), prod_r, prod_i, diag, partner_of(0))
    state = lax.fori_loop(0, SWEEPS * (count - 1), advance, state, unroll=3)
    vec_r, vec_i, _, _, eigen, _ = state
    sum_r = jnp.sum(vec_r, axis=0, keepdims=True)
    sum_i = jnp.sum(vec_i, axis=0, keepdims=True)
    magnitude = jnp.sqrt(sum_r * sum_r + sum_i * sum_i)
    scaling = 1.0 / (jnp.maximum(magnitude, 1.0) * jnp.sqrt(count * (eigen + 1e-06)))
    phase_r = sum_r * scaling
    phase_i = -sum_i * scaling
    coef = jnp.where(
        in_real, vec_r * phase_r - vec_i * phase_i, vec_r * phase_i + vec_i * phase_r
    )
    return coef, eigen


def signed_wave(base, index):
    lanes = base.shape[1]
    value = lane_gather(base, jnp.bitwise_and(index, lanes - 1))
    return jnp.where(jnp.bitwise_and(index, lanes) == 0, value, -value)


def write_table(table_ref, offsets_ref, freqs_ref, me, groups, owners):
    rows, nfft = table_ref.shape
    half = nfft // 2
    lane = lax.broadcasted_iota(jnp.int32, (8, half), 1)
    sub = lax.broadcasted_iota(jnp.int32, (8, half), 0)
    base = jnp.cos(2.0 * math.pi / nfft * lane.astype(jnp.float32))
    own = offsets_ref[me]
    before = jnp.where(me > 0, offsets_ref[jnp.maximum(me - 1, 0)], 0)
    quarter = jnp.where(lax.rem(sub, 2) == 1, nfft // 4, 0)
    windows = {}
    for tile in range(rows // 8):
        tile_rows = range(8 * tile, 8 * tile + 8)
        pieces = tuple(r % (4 * groups) // (2 * groups) for r in tile_rows)
        freq = [owners[r // (4 * groups)] * groups + r % (2 * groups) // 2 for r in tile_rows]
        freq_rows = jnp.full((8, half), freqs_ref[freq[0]], jnp.int32)
        for s in range(2, 8, 2):
            freq_rows = jnp.where(sub >= s, freqs_ref[freq[s]], freq_rows)
        if pieces not in windows:
            tail = jnp.zeros((8, half), jnp.bool_)
            for s in range(8):
                if pieces[s]:
                    tail = tail | (sub == s)
            start = jnp.where(tail, before, own)
            window = []
            for h in range(2):
                lag = lane + h * half - start
                hann = 0.5 - 0.5 * signed_wave(base, lag)
                valid = (tail & (lag < 0)) | (jnp.logical_not(tail) & (lag >= 0))
                window.append((lag, jnp.where(valid, hann, 0.0) / math.sqrt(nfft)))
            windows[pieces] = window
        for h in range(2):
            lag, factor = windows[pieces][h]
            wave = signed_wave(base, freq_rows * lag + quarter)
            table_ref[8 * tile : 8 * tile + 8, h * half : (h + 1) * half] = factor * wave


def pipeline_kernel(
    nblocks, npart, groups, scale, energy,
    snaps_ref, weights_ref, offsets_ref, freqs_ref, modes_ref, spectrum_ref,
    table, stage, recv, spectra, gram_part, total_part,
    send_sem, recv_sem, gram_send, gram_recv, total_send, total_recv,
):
    me = lax.axis_index("blk")
    side = lax.axis_index("pts")
    nvars, nfft, npts = snaps_ref.shape
    rows = 2 * groups * nblocks
    half = rows // 2
    piece = 2 * groups

    def block_peer(k):
        return lax.rem(me + k, nblocks)

    def side_peer(k):
        return lax.rem(side + k, npart)

    barrier = pltpu.get_barrier_semaphore()
    for k in range(1, nblocks):
        pl.semaphore_signal(barrier, inc=1, device_id={"blk": block_peer(k)}, device_id_type=MESH)
    for k in range(1, npart):
        pl.semaphore_signal(barrier, inc=1, device_id={"pts": side_peer(k)}, device_id_type=MESH)

    order = sorted(range(nblocks), key=lambda k: abs(k - nblocks // 2))
    write_table(table, offsets_ref, freqs_ref, me, groups, [block_peer(k) for k in order])
    snaps = jnp.concatenate([snaps_ref[v] for v in range(nvars)], axis=1)

    def spectra_copy(place, slot):
        return pltpu.make_async_remote_copy(
            src_ref=stage.at[place], dst_ref=recv.at[slot], send_sem=send_sem.at[place],
            recv_sem=recv_sem.at[slot], device_id={"blk": block_peer(order[place])},
            device_id_type=MESH,
        )

    share = nblocks // CHUNKS
    for chunk in range(CHUNKS):
        places = range(chunk * share, (chunk + 1) * share)
        part = jnp.dot(
            table[2 * piece * places[0] : 2 * piece * (places[-1] + 1), :], snaps,
            precision=lax.Precision.HIGH, preferred_element_type=jnp.float32,
        )
        for at, place in enumerate(places):
            stage[place] = part[2 * piece * at : 2 * piece * (at + 1)]
        if chunk == 0:
            pl.semaphore_wait(barrier, nblocks - 1 + npart - 1)
        for place in places:
            if order[place]:
                spectra_copy(place, me).start()
    recv[me] = stage[order.index(0)]
    recv[nblocks] = jnp.zeros(recv.shape[1:], jnp.float32)
    for place in range(nblocks):
        if order[place]:
            spectra_copy(place, block_peer(nblocks - order[place])).wait_recv()

    for ri in range(2):
        for f in range(groups):
            at = (ri * groups + f) * nblocks
            own = recv[0:nblocks, 2 * f + ri, :]
            tail = recv[1 : nblocks + 1, piece + 2 * f + ri, :]
            spectra[at : at + nblocks, :] = own + tail

    weight = jnp.concatenate([weights_ref[v : v + 1, :] for v in range(nvars)], axis=1)
    gram_all = lax.dot_general(
        spectra[...] * weight, spectra[...], (((1,), (1,)), ((), ())),
        precision=HIGH, preferred_element_type=jnp.float32,
    )
    lane = lax.broadcasted_iota(jnp.int32, (1, rows), 1)
    sign = jnp.where(lane < half, 1.0, -1.0).astype(jnp.float32)
    group_of = lax.rem(lane, half) // nblocks
    gram = jnp.zeros((nblocks, rows), jnp.float32)
    for f in range(groups):
        upper = gram_all[f * nblocks : (f + 1) * nblocks]
        lower = gram_all[half + f * nblocks : half + (f + 1) * nblocks]
        gram = jnp.where(group_of == f, upper + sign * pltpu.roll(lower, half, 1), gram)
    gram_part[side] = gram * scale

    def gram_copy(k, slot):
        peer = side_peer(k)
        return pltpu.make_async_remote_copy(
            src_ref=gram_part.at[side], dst_ref=gram_part.at[slot], send_sem=gram_send.at[k],
            recv_sem=gram_recv.at[slot], device_id={"pts": peer}, device_id_type=MESH,
        )

    for k in range(1, npart):
        gram_copy(k, side).start()
    for k in range(1, npart):
        gram_copy(k, side_peer(k)).wait_recv()
    gram = gram_part[0]
    for k in range(1, npart):
        gram = gram + gram_part[k]

    row = lax.broadcasted_iota(jnp.int32, (nblocks, rows), 0)
    trace = jnp.where((row == lax.rem(lane, nblocks)) & (lane < half), gram, 0.0)
    trace = jnp.sum(jnp.sum(trace, axis=0, keepdims=True), axis=1, keepdims=True)
    total_part[me] = jnp.broadcast_to(trace, total_part.shape[1:])

    def total_copy(k, slot):
        peer = block_peer(k)
        return pltpu.make_async_remote_copy(
            src_ref=total_part.at[me], dst_ref=total_part.at[slot], send_sem=total_send.at[k],
            recv_sem=total_recv.at[slot], device_id={"blk": peer}, device_id_type=MESH,
        )

    for k in range(1, nblocks):
        total_copy(k, me).start()

    coef, eigen = jacobi_on_lanes(gram, nblocks, groups)

    turned = -sign * half_turned(coef, half)
    pieces = [jnp.where(group_of == f, block, 0.0) for block in (coef, turned) for f in range(groups)]
    mixing = jnp.concatenate(pieces, axis=0).T
    modes_ref[...] = jnp.dot(
        mixing, spectra[...], precision=lax.Precision.HIGH, preferred_element_type=jnp.float32
    )

    for k in range(1, nblocks):
        total_copy(k, block_peer(k)).wait_recv()
    total = jnp.sum(total_part[...], axis=0)
    share_of = energy * eigen / total[:1]
    for f in range(groups):
        spectrum_ref[f : f + 1, :] = share_of[:, f * nblocks : (f + 1) * nblocks]
    for place in range(nblocks):
        if order[place]:
            spectra_copy(place, me).wait_send()
    for k in range(1, nblocks):
        total_copy(k, me).wait_send()
    for k in range(1, npart):
        gram_copy(k, side).wait_send()


def body(snapshots, weights, offsets, freqs):
    nfft, nvars, npts = snapshots.shape
    nfreq = freqs.shape[0]
    nblocks = lax.axis_size("blk")
    npart = lax.axis_size("pts")
    groups = nfreq // nblocks
    width = nvars * npts
    rows = 2 * nfreq
    scale = 1.0 / (nblocks * nvars * npts * npart)
    dma = pltpu.SemaphoreType.DMA
    vmem = pl.BlockSpec(memory_space=pltpu.VMEM)
    smem = pl.BlockSpec(memory_space=pltpu.SMEM)
    modes, spectrum = pl.pallas_call(
        functools.partial(pipeline_kernel, nblocks, npart, groups, scale, float(nfreq * nblocks)),
        out_shape=(
            jax.ShapeDtypeStruct((rows, width), jnp.float32),
            jax.ShapeDtypeStruct((groups, nblocks), jnp.float32),
        ),
        in_specs=[vmem, vmem, smem, smem],
        out_specs=(vmem, vmem),
        scratch_shapes=[
            pltpu.VMEM((2 * rows, nfft), jnp.float32),
            pltpu.VMEM((nblocks, 4 * groups, width), jnp.float32),
            pltpu.VMEM((nblocks + 1, 4 * groups, width), jnp.float32),
            pltpu.VMEM((rows, width), jnp.float32),
            pltpu.VMEM((npart, nblocks, rows), jnp.float32),
            pltpu.VMEM((nblocks, 8, rows), jnp.float32),
            dma((nblocks,)), dma((nblocks,)),
            dma((npart,)), dma((npart,)),
            dma((nblocks,)), dma((nblocks,)),
        ],
        compiler_params=pltpu.CompilerParams(
            collective_id=0, has_side_effects=True, vmem_limit_bytes=32 * 1024 * 1024
        ),
    )(snapshots.transpose(1, 0, 2), weights, offsets, freqs)
    modes = modes.reshape(2, groups, nblocks, nvars, npts).transpose(1, 2, 0, 3, 4)
    return modes, spectrum


def solution(mesh):
    return jax.shard_map(
        body,
        mesh=mesh,
        in_specs=(P("blk", None, "pts"), P(None, "pts"), P(), P()),
        out_specs=(P("blk", None, None, None, "pts"), P("blk", None)),
        check_vma=False,
    )
```

```python
import functools
import math

import jax
import jax.numpy as jnp
from jax import lax
from jax.experimental import pallas as pl
from jax.experimental.pallas import tpu as pltpu
from jax.sharding import PartitionSpec as P

SWEEPS = 2


HIGH = lax.Precision.HIGHEST
DAMPING = 0.01
CHUNKS = 2
MESH = pl.DeviceIdType.MESH


def half_turned(row, half):
    return pltpu.roll(row, half, 1)


def lane_gather(block, index):
    rows = max(block.shape[0], 8)
    wide = jnp.broadcast_to(block, (rows, block.shape[1]))
    index = index if index.shape == wide.shape else jnp.broadcast_to(index[:1], wide.shape)
    return jnp.take_along_axis(wide, index, axis=1, mode="promise_in_bounds")[: block.shape[0]]


def jacobi_on_lanes(gram, count, groups):
    half = groups * count
    lanes = 2 * half
    lane = lax.broadcasted_iota(jnp.int32, (8, lanes), 1)
    column = lax.rem(lane, count)
    first = lane - column
    in_real = lane[:1] < half
    row = lax.broadcasted_iota(jnp.int32, (count, lanes), 0)
    eye = jnp.where(row == column[:1], 1.0, 0.0).astype(jnp.float32)
    turned = half_turned(gram, half)
    prod_r = jnp.where(in_real, gram, turned)
    prod_i = jnp.where(in_real, turned, gram)
    diag = jnp.sum(prod_r * eye, axis=0, keepdims=True)

    def partner_of(turn):
        mirror = 2 * turn - column
        mirror = jnp.where(mirror < 0, mirror + (count - 1), mirror)
        mirror = jnp.where(mirror >= count - 1, mirror - (count - 1), mirror)
        return jnp.where(column == count - 1, turn, jnp.where(column == turn, count - 1, mirror))

    def advance(counter, carry):
        vec_r, vec_i, prod_r, prod_i, diag, partner = carry
        following = partner_of(lax.rem(counter + 1, count - 1))
        parity = jnp.where(column < partner, 1.0, -1.0).astype(jnp.float32)[:1]
        same = first + partner
        prod_sr = lane_gather(prod_r, same)
        prod_si = lane_gather(prod_i, same)
        diag_pair = lane_gather(diag, same)
        vec_sr = lane_gather(vec_r, same)
        vec_si = lane_gather(vec_i, same)
        pair_real = jnp.sum(vec_r * prod_sr + vec_i * prod_si, axis=0, keepdims=True)
        pair_imag = jnp.sum(vec_r * prod_si - vec_i * prod_sr, axis=0, keepdims=True)
        delta = parity * (diag_pair - diag)
        size4 = 4.0 * (pair_real * pair_real + pair_imag * pair_imag)
        radius = jnp.sqrt(delta * delta + size4)
        upper = radius + (delta + DAMPING * (diag + diag_pair))
        inverse = lax.rsqrt(upper * upper + size4)
        cosine = upper * inverse
        scale = 2.0 * parity * inverse
        coef_r = -scale * pair_real
        coef_i = scale * pair_imag
        sine_sq = size4 * inverse * inverse
        diag = cosine * cosine * diag + sine_sq * diag_pair - parity * cosine * size4 * inverse

        def turn_pair(real, imag, swap_real, swap_imag):
            return (
                real * cosine + (swap_real * coef_r - swap_imag * coef_i),
                imag * cosine + (swap_real * coef_i + swap_imag * coef_r),
            )

        prod_r, prod_i = turn_pair(prod_r, prod_i, prod_sr, prod_si)
        vec_r, vec_i = turn_pair(vec_r, vec_i, vec_sr, vec_si)
        return vec_r, vec_i, prod_r, prod_i, diag, following

    state = (eye, jnp.zeros_like(eye), prod_r, prod_i, diag, partner_of(0))
    state = lax.fori_loop(0, SWEEPS * (count - 1), advance, state, unroll=3)
    vec_r, vec_i, _, _, eigen, _ = state
    sum_r = jnp.sum(vec_r, axis=0, keepdims=True)
    sum_i = jnp.sum(vec_i, axis=0, keepdims=True)
    magnitude = jnp.sqrt(sum_r * sum_r + sum_i * sum_i)
    scaling = 1.0 / (jnp.maximum(magnitude, 1.0) * jnp.sqrt(count * (eigen + 1e-06)))
    phase_r = sum_r * scaling
    phase_i = -sum_i * scaling
    coef = jnp.where(
        in_real, vec_r * phase_r - vec_i * phase_i, vec_r * phase_i + vec_i * phase_r
    )
    return coef, eigen


def signed_wave(base, index):
    lanes = base.shape[1]
    value = lane_gather(base, jnp.bitwise_and(index, lanes - 1))
    return jnp.where(jnp.bitwise_and(index, lanes) == 0, value, -value)


def write_table(table_ref, offsets_ref, freqs_ref, me, groups, owners):
    rows, nfft = table_ref.shape
    half = nfft // 2
    lane = lax.broadcasted_iota(jnp.int32, (8, half), 1)
    sub = lax.broadcasted_iota(jnp.int32, (8, half), 0)
    base = jnp.cos(2.0 * math.pi / nfft * lane.astype(jnp.float32))
    own = offsets_ref[me]
    before = jnp.where(me > 0, offsets_ref[jnp.maximum(me - 1, 0)], 0)
    quarter = jnp.where(lax.rem(sub, 2) == 1, nfft // 4, 0)
    windows = {}
    for tile in range(rows // 8):
        tile_rows = range(8 * tile, 8 * tile + 8)
        pieces = tuple(r % (4 * groups) // (2 * groups) for r in tile_rows)
        freq = [owners[r // (4 * groups)] * groups + r % (2 * groups) // 2 for r in tile_rows]
        freq_rows = jnp.full((8, half), freqs_ref[freq[0]], jnp.int32)
        for s in range(2, 8, 2):
            freq_rows = jnp.where(sub >= s, freqs_ref[freq[s]], freq_rows)
        if pieces not in windows:
            tail = jnp.zeros((8, half), jnp.bool_)
            for s in range(8):
                if pieces[s]:
                    tail = tail | (sub == s)
            start = jnp.where(tail, before, own)
            window = []
            for h in range(2):
                lag = lane + h * half - start
                hann = 0.5 - 0.5 * signed_wave(base, lag)
                valid = (tail & (lag < 0)) | (jnp.logical_not(tail) & (lag >= 0))
                window.append((lag, jnp.where(valid, hann, 0.0) / math.sqrt(nfft)))
            windows[pieces] = window
        for h in range(2):
            lag, factor = windows[pieces][h]
            wave = signed_wave(base, freq_rows * lag + quarter)
            table_ref[8 * tile : 8 * tile + 8, h * half : (h + 1) * half] = factor * wave


def pipeline_kernel(
    nblocks, npart, groups, scale, energy,
    snaps_hbm, weights_hbm, offsets_hbm, freqs_hbm, modes_ref, spectrum_ref,
    snaps_ref, weights_ref, offsets_ref, freqs_ref,
    table, stage, recv, halo, spectra, gram_part, total_part,
    input_sem, send_sem, recv_sem, halo_send, halo_recv, extra_send, extra_recv,
    gram_send, gram_recv, total_send, total_recv,
):
    inputs = [
        pltpu.make_async_copy(src, dst, input_sem.at[i])
        for i, (src, dst) in enumerate((
            (offsets_hbm, offsets_ref), (freqs_hbm, freqs_ref),
            (snaps_hbm, snaps_ref), (weights_hbm, weights_ref),
        ))
    ]
    for copy in inputs:
        copy.start()
    me = lax.axis_index("blk")
    side = lax.axis_index("pts")
    nvars, nfft, npts = snaps_ref.shape
    rows = 2 * groups * nblocks
    half = rows // 2
    piece = 2 * groups
    reach = nblocks // 2
    upper_half = me // reach
    within = lax.rem(me, reach)
    far_base = (1 - upper_half) * reach
    near_base = upper_half * reach
    far = [far_base + lax.rem(within + j, reach) for j in range(reach)]
    near = [near_base + lax.rem(within + j, reach) for j in range(reach)]
    owners = far + near

    def block_peer(k):
        return lax.rem(me + k, nblocks)

    def side_peer(k):
        return lax.rem(side + k, npart)

    barrier = pltpu.get_barrier_semaphore()
    for k in range(1, nblocks):
        pl.semaphore_signal(barrier, inc=1, device_id={"blk": block_peer(k)}, device_id_type=MESH)
    for k in range(1, npart):
        pl.semaphore_signal(barrier, inc=1, device_id={"pts": side_peer(k)}, device_id_type=MESH)

    inputs[0].wait()
    inputs[1].wait()
    write_table(table, offsets_ref, freqs_ref, me, groups, owners)
    inputs[2].wait()
    snaps = jnp.concatenate([snaps_ref[v] for v in range(nvars)], axis=1)

    def transform(first):
        part = jnp.dot(
            table[2 * piece * first : 2 * piece * (first + reach), :], snaps,
            precision=lax.Precision.HIGH, preferred_element_type=jnp.float32,
        )
        for j in range(reach):
            at = 2 * piece * j
            stage[first + j, 0] = part[at : at + piece]
            stage[first + j, 1] = part[at + piece : at + 2 * piece]

    def remote(src, dst, sent, received, peer):
        return pltpu.make_async_remote_copy(
            src_ref=src, dst_ref=dst, send_sem=sent, recv_sem=received,
            device_id={"blk": peer}, device_id_type=MESH,
        )

    share = reach // CHUNKS
    before = jnp.maximum(me - 1, 0)
    after = jnp.minimum(me + 1, nblocks - 1)

    def halo_copy(chunk, peer):
        places = pl.ds(chunk * share, share)
        return remote(
            stage.at[places, 1], halo.at[places], halo_send.at[chunk], halo_recv.at[chunk], peer
        )

    def far_copy(j, slot, peer):
        return remote(stage.at[j, 0], recv.at[slot, 0], send_sem.at[j], recv_sem.at[slot], peer)

    def near_copy(j, slot, peer):
        at = reach + j
        return remote(stage.at[at], recv.at[slot], send_sem.at[at], recv_sem.at[slot], peer)

    def extra_copy(j):
        return remote(stage.at[j, 1], recv.at[reach, 1], extra_send.at[j], extra_recv.at[0], far[j])

    transform(0)
    pl.semaphore_wait(barrier, nblocks - 1 + npart - 1)

    @pl.when(within != 0)
    def _():
        for chunk in range(CHUNKS):
            halo_copy(chunk, before).start()

    @pl.when(me == reach)
    def _():
        for j in range(reach):
            extra_copy(j).start()

    transform(reach)
    for chunk in range(CHUNKS):
        places = [(chunk * share + i, (chunk * share + i + 1) % reach) for i in range(share)]

        @pl.when(within != reach - 1)
        def _():
            halo_copy(chunk, after).wait_recv()
            for theirs, mine in places:
                stage[mine, 0] = stage[mine, 0] + halo[theirs]

        for _, mine in places:
            far_copy(mine, me, far[mine]).start()
    for j in range(1, reach):
        near_copy(j, me, near[j]).start()

    recv[me] = stage[reach]
    empty = jnp.zeros(recv.shape[2:], jnp.float32)
    recv[nblocks, 1] = empty
    for i in range(1, reach):
        recv[far_base + i, 1] = empty

    @pl.when(upper_half == 1)
    def _():
        recv[0, 1] = empty

    @pl.when(upper_half == 0)
    def _():
        extra_copy(0).wait_recv()

    for j in range(reach):
        far_copy(j, far[j], far[j]).wait_recv()
    for j in range(1, reach):
        near_copy(j, near[j], near[j]).wait_recv()
    inputs[3].wait()

    for ri in range(2):
        for f in range(groups):
            at = (ri * groups + f) * nblocks
            own = recv[0:nblocks, 0, 2 * f + ri, :]
            tail = recv[1 : nblocks + 1, 1, 2 * f + ri, :]
            spectra[at : at + nblocks, :] = own + tail

    weight = jnp.concatenate([weights_ref[v : v + 1, :] for v in range(nvars)], axis=1)
    gram_all = lax.dot_general(
        spectra[...] * weight, spectra[...], (((1,), (1,)), ((), ())),
        precision=HIGH, preferred_element_type=jnp.float32,
    )
    lane = lax.broadcasted_iota(jnp.int32, (1, rows), 1)
    sign = jnp.where(lane < half, 1.0, -1.0).astype(jnp.float32)
    group_of = lax.rem(lane, half) // nblocks
    gram = jnp.zeros((nblocks, rows), jnp.float32)
    for f in range(groups):
        upper = gram_all[f * nblocks : (f + 1) * nblocks]
        lower = gram_all[half + f * nblocks : half + (f + 1) * nblocks]
        gram = jnp.where(group_of == f, upper + sign * pltpu.roll(lower, half, 1), gram)
    gram_part[side] = gram * scale

    def gram_copy(k, slot):
        peer = side_peer(k)
        return pltpu.make_async_remote_copy(
            src_ref=gram_part.at[side], dst_ref=gram_part.at[slot], send_sem=gram_send.at[k],
            recv_sem=gram_recv.at[slot], device_id={"pts": peer}, device_id_type=MESH,
        )

    for k in range(1, npart):
        gram_copy(k, side).start()
    for k in range(1, npart):
        gram_copy(k, side_peer(k)).wait_recv()
    gram = gram_part[0]
    for k in range(1, npart):
        gram = gram + gram_part[k]

    row = lax.broadcasted_iota(jnp.int32, (nblocks, rows), 0)
    trace = jnp.where((row == lax.rem(lane, nblocks)) & (lane < half), gram, 0.0)
    trace = jnp.sum(jnp.sum(trace, axis=0, keepdims=True), axis=1, keepdims=True)
    total_part[me] = jnp.broadcast_to(trace, total_part.shape[1:])

    def total_copy(k, slot):
        peer = block_peer(k)
        return pltpu.make_async_remote_copy(
            src_ref=total_part.at[me], dst_ref=total_part.at[slot], send_sem=total_send.at[k],
            recv_sem=total_recv.at[slot], device_id={"blk": peer}, device_id_type=MESH,
        )

    for k in range(1, nblocks):
        total_copy(k, me).start()

    coef, eigen = jacobi_on_lanes(gram, nblocks, groups)

    turned = -sign * half_turned(coef, half)
    pieces = [jnp.where(group_of == f, block, 0.0) for block in (coef, turned) for f in range(groups)]
    mixing = jnp.concatenate(pieces, axis=0).T
    modes_ref[...] = jnp.dot(
        mixing, spectra[...], precision=lax.Precision.HIGH, preferred_element_type=jnp.float32
    )

    for k in range(1, nblocks):
        total_copy(k, block_peer(k)).wait_recv()
    total = jnp.sum(total_part[...], axis=0)
    share_of = energy * eigen / total[:1]
    for f in range(groups):
        spectrum_ref[f : f + 1, :] = share_of[:, f * nblocks : (f + 1) * nblocks]
    for j in range(reach):
        far_copy(j, me, far[j]).wait_send()
    for j in range(1, reach):
        near_copy(j, me, near[j]).wait_send()

    @pl.when(within != 0)
    def _():
        for chunk in range(CHUNKS):
            halo_copy(chunk, before).wait_send()

    @pl.when(me == reach)
    def _():
        for j in range(reach):
            extra_copy(j).wait_send()

    for k in range(1, nblocks):
        total_copy(k, me).wait_send()
    for k in range(1, npart):
        gram_copy(k, side).wait_send()


def body(snapshots, weights, offsets, freqs):
    nfft, nvars, npts = snapshots.shape
    nfreq = freqs.shape[0]
    nblocks = lax.axis_size("blk")
    npart = lax.axis_size("pts")
    groups = nfreq // nblocks
    width = nvars * npts
    rows = 2 * nfreq
    scale = 1.0 / (nblocks * nvars * npts * npart)
    dma = pltpu.SemaphoreType.DMA
    vmem = pl.BlockSpec(memory_space=pltpu.VMEM)
    far_memory = pl.BlockSpec(memory_space=pltpu.HBM)
    modes, spectrum = pl.pallas_call(
        functools.partial(pipeline_kernel, nblocks, npart, groups, scale, float(nfreq * nblocks)),
        out_shape=(
            jax.ShapeDtypeStruct((rows, width), jnp.float32),
            jax.ShapeDtypeStruct((groups, nblocks), jnp.float32),
        ),
        in_specs=[far_memory] * 4,
        out_specs=(vmem, vmem),
        scratch_shapes=[
            pltpu.VMEM((nvars, nfft, npts), jnp.float32),
            pltpu.VMEM((nvars, npts), jnp.float32),
            pltpu.SMEM((nblocks,), jnp.int32),
            pltpu.SMEM((nfreq,), jnp.int32),
            pltpu.VMEM((2 * rows, nfft), jnp.float32),
            pltpu.VMEM((nblocks, 2, 2 * groups, width), jnp.float32),
            pltpu.VMEM((nblocks + 1, 2, 2 * groups, width), jnp.float32),
            pltpu.VMEM((nblocks // 2, 2 * groups, width), jnp.float32),
            pltpu.VMEM((rows, width), jnp.float32),
            pltpu.VMEM((npart, nblocks, rows), jnp.float32),
            pltpu.VMEM((nblocks, 8, rows), jnp.float32),
            dma((4,)),
            dma((nblocks,)), dma((nblocks,)),
            dma((CHUNKS,)), dma((CHUNKS,)),
            dma((nblocks // 2,)), dma((1,)),
            dma((npart,)), dma((npart,)),
            dma((nblocks,)), dma((nblocks,)),
        ],
        compiler_params=pltpu.CompilerParams(
            collective_id=0, has_side_effects=True, vmem_limit_bytes=32 * 1024 * 1024
        ),
    )(snapshots.transpose(1, 0, 2), weights, offsets, freqs)
    modes = modes.reshape(2, groups, nblocks, nvars, npts).transpose(1, 2, 0, 3, 4)
    return modes, spectrum


def solution(mesh):
    return jax.shard_map(
        body,
        mesh=mesh,
        in_specs=(P("blk", None, "pts"), P(None, "pts"), P(), P()),
        out_specs=(P("blk", None, None, None, "pts"), P("blk", None)),
        check_vma=False,
    )
```

```python
import functools
import math

import jax
import jax.numpy as jnp
from jax import lax
from jax.experimental import pallas as pl
from jax.experimental.pallas import tpu as pltpu
from jax.sharding import PartitionSpec as P

SWEEPS = 2


HIGH = lax.Precision.HIGHEST
DAMPING = 0.01
CHUNKS = 2
MESH = pl.DeviceIdType.MESH


def half_turned(row, half):
    return pltpu.roll(row, half, 1)


def lane_gather(block, index):
    rows = max(block.shape[0], 8)
    wide = jnp.broadcast_to(block, (rows, block.shape[1]))
    index = index if index.shape == wide.shape else jnp.broadcast_to(index[:1], wide.shape)
    return jnp.take_along_axis(wide, index, axis=1, mode="promise_in_bounds")[: block.shape[0]]


def jacobi_on_lanes(gram, count, groups):
    half = groups * count
    lanes = 2 * half
    lane = lax.broadcasted_iota(jnp.int32, (8, lanes), 1)
    column = lax.rem(lane, count)
    first = lane - column
    in_real = lane[:1] < half
    row = lax.broadcasted_iota(jnp.int32, (count, lanes), 0)
    eye = jnp.where(row == column[:1], 1.0, 0.0).astype(jnp.float32)
    turned = half_turned(gram, half)
    prod_r = jnp.where(in_real, gram, turned)
    prod_i = jnp.where(in_real, turned, gram)
    diag = jnp.sum(prod_r * eye, axis=0, keepdims=True)

    def partner_of(turn):
        mirror = 2 * turn - column
        mirror = jnp.where(mirror < 0, mirror + (count - 1), mirror)
        mirror = jnp.where(mirror >= count - 1, mirror - (count - 1), mirror)
        return jnp.where(column == count - 1, turn, jnp.where(column == turn, count - 1, mirror))

    def advance(counter, carry):
        vec_r, vec_i, prod_r, prod_i, diag, partner = carry
        following = partner_of(lax.rem(counter + 1, count - 1))
        parity = jnp.where(column < partner, 1.0, -1.0).astype(jnp.float32)[:1]
        same = first + partner
        prod_sr = lane_gather(prod_r, same)
        prod_si = lane_gather(prod_i, same)
        diag_pair = lane_gather(diag, same)
        vec_sr = lane_gather(vec_r, same)
        vec_si = lane_gather(vec_i, same)
        pair_real = jnp.sum(vec_r * prod_sr + vec_i * prod_si, axis=0, keepdims=True)
        pair_imag = jnp.sum(vec_r * prod_si - vec_i * prod_sr, axis=0, keepdims=True)
        delta = parity * (diag_pair - diag)
        size4 = 4.0 * (pair_real * pair_real + pair_imag * pair_imag)
        radius = jnp.sqrt(delta * delta + size4)
        upper = radius + (delta + DAMPING * (diag + diag_pair))
        inverse = lax.rsqrt(upper * upper + size4)
        cosine = upper * inverse
        scale = 2.0 * parity * inverse
        coef_r = -scale * pair_real
        coef_i = scale * pair_imag
        sine_sq = size4 * inverse * inverse
        diag = cosine * cosine * diag + sine_sq * diag_pair - parity * cosine * size4 * inverse

        def turn_pair(real, imag, swap_real, swap_imag):
            return (
                real * cosine + (swap_real * coef_r - swap_imag * coef_i),
                imag * cosine + (swap_real * coef_i + swap_imag * coef_r),
            )

        prod_r, prod_i = turn_pair(prod_r, prod_i, prod_sr, prod_si)
        vec_r, vec_i = turn_pair(vec_r, vec_i, vec_sr, vec_si)
        return vec_r, vec_i, prod_r, prod_i, diag, following

    state = (eye, jnp.zeros_like(eye), prod_r, prod_i, diag, partner_of(0))
    state = lax.fori_loop(0, SWEEPS * (count - 1), advance, state, unroll=3)
    vec_r, vec_i, _, _, eigen, _ = state
    sum_r = jnp.sum(vec_r, axis=0, keepdims=True)
    sum_i = jnp.sum(vec_i, axis=0, keepdims=True)
    magnitude = jnp.sqrt(sum_r * sum_r + sum_i * sum_i)
    scaling = 1.0 / (jnp.maximum(magnitude, 1.0) * jnp.sqrt(count * (eigen + 1e-06)))
    phase_r = sum_r * scaling
    phase_i = -sum_i * scaling
    coef = jnp.where(
        in_real, vec_r * phase_r - vec_i * phase_i, vec_r * phase_i + vec_i * phase_r
    )
    return coef, eigen


def signed_wave(base, index):
    lanes = base.shape[1]
    value = lane_gather(base, jnp.bitwise_and(index, lanes - 1))
    return jnp.where(jnp.bitwise_and(index, lanes) == 0, value, -value)


def write_table(table_ref, offsets_ref, freqs_ref, me, groups, owners):
    rows, nfft = table_ref.shape
    half = nfft // 2
    lane = lax.broadcasted_iota(jnp.int32, (8, half), 1)
    sub = lax.broadcasted_iota(jnp.int32, (8, half), 0)
    base = jnp.cos(2.0 * math.pi / nfft * lane.astype(jnp.float32))
    own = offsets_ref[me]
    before = jnp.where(me > 0, offsets_ref[jnp.maximum(me - 1, 0)], 0)
    quarter = jnp.where(lax.rem(sub, 2) == 1, nfft // 4, 0)
    windows = {}
    for tile in range(rows // 8):
        tile_rows = range(8 * tile, 8 * tile + 8)
        pieces = tuple(r % (4 * groups) // (2 * groups) for r in tile_rows)
        freq = [owners[r // (4 * groups)] * groups + r % (2 * groups) // 2 for r in tile_rows]
        freq_rows = jnp.full((8, half), freqs_ref[freq[0]], jnp.int32)
        for s in range(2, 8, 2):
            freq_rows = jnp.where(sub >= s, freqs_ref[freq[s]], freq_rows)
        if pieces not in windows:
            tail = jnp.zeros((8, half), jnp.bool_)
            for s in range(8):
                if pieces[s]:
                    tail = tail | (sub == s)
            start = jnp.where(tail, before, own)
            window = []
            for h in range(2):
                lag = lane + h * half - start
                hann = 0.5 - 0.5 * signed_wave(base, lag)
                valid = (tail & (lag < 0)) | (jnp.logical_not(tail) & (lag >= 0))
                window.append((lag, jnp.where(valid, hann, 0.0) / math.sqrt(nfft)))
            windows[pieces] = window
        for h in range(2):
            lag, factor = windows[pieces][h]
            wave = signed_wave(base, freq_rows * lag + quarter)
            table_ref[8 * tile : 8 * tile + 8, h * half : (h + 1) * half] = factor * wave


def pipeline_kernel(
    nblocks, npart, groups, scale, energy,
    snaps_hbm, weights_hbm, offsets_hbm, freqs_hbm, modes_ref, spectrum_ref,
    snaps_ref, weights_ref, offsets_ref, freqs_ref,
    table, stage, recv, halo, spectra, order, gram_part, total_part,
    input_sem, send_sem, recv_sem, halo_send, halo_recv, extra_send, extra_recv,
    gram_send, gram_recv, total_send, total_recv,
):
    inputs = [
        pltpu.make_async_copy(src, dst, input_sem.at[i])
        for i, (src, dst) in enumerate((
            (offsets_hbm, offsets_ref), (freqs_hbm, freqs_ref),
            (snaps_hbm, snaps_ref), (weights_hbm, weights_ref),
        ))
    ]
    for copy in inputs:
        copy.start()
    me = lax.axis_index("blk")
    side = lax.axis_index("pts")
    nvars, nfft, npts = snaps_ref.shape
    rows = 2 * groups * nblocks
    half = rows // 2
    piece = 2 * groups
    reach = nblocks // 2
    upper_half = me // reach
    within = lax.rem(me, reach)
    far_base = (1 - upper_half) * reach
    near_base = upper_half * reach
    far = [far_base + lax.rem(within + j, reach) for j in range(reach)]
    near = [near_base + lax.rem(within + j, reach) for j in range(reach)]
    owners = far + near

    def block_peer(k):
        return lax.rem(me + k, nblocks)

    def side_peer(k):
        return lax.rem(side + k, npart)

    barrier = pltpu.get_barrier_semaphore()
    for k in range(1, nblocks):
        pl.semaphore_signal(barrier, inc=1, device_id={"blk": block_peer(k)}, device_id_type=MESH)
    for k in range(1, npart):
        pl.semaphore_signal(barrier, inc=1, device_id={"pts": side_peer(k)}, device_id_type=MESH)

    inputs[0].wait()
    inputs[1].wait()
    write_table(table, offsets_ref, freqs_ref, me, groups, owners)
    inputs[2].wait()
    snaps = jnp.concatenate([snaps_ref[v] for v in range(nvars)], axis=1)

    def transform(first):
        part = jnp.dot(
            table[2 * piece * first : 2 * piece * (first + reach), :], snaps,
            precision=lax.Precision.HIGH, preferred_element_type=jnp.float32,
        )
        for j in range(reach):
            at = 2 * piece * j
            stage[first + j, 0] = part[at : at + piece]
            stage[first + j, 1] = part[at + piece : at + 2 * piece]

    def remote(src, dst, sent, received, peer):
        return pltpu.make_async_remote_copy(
            src_ref=src, dst_ref=dst, send_sem=sent, recv_sem=received,
            device_id={"blk": peer}, device_id_type=MESH,
        )

    share = reach // CHUNKS
    before = jnp.maximum(me - 1, 0)
    after = jnp.minimum(me + 1, nblocks - 1)

    def halo_copy(chunk, peer):
        places = pl.ds(chunk * share, share)
        return remote(
            stage.at[places, 1], halo.at[places], halo_send.at[chunk], halo_recv.at[chunk], peer
        )

    def far_copy(j, slot, peer):
        return remote(stage.at[j, 0], recv.at[slot, 0], send_sem.at[j], recv_sem.at[slot], peer)

    def near_copy(j, slot, peer):
        at = reach + j
        return remote(stage.at[at], recv.at[slot], send_sem.at[at], recv_sem.at[slot], peer)

    def extra_copy(j):
        return remote(stage.at[j, 1], recv.at[reach, 1], extra_send.at[j], extra_recv.at[0], far[j])

    transform(0)
    pl.semaphore_wait(barrier, nblocks - 1 + npart - 1)

    @pl.when(within != 0)
    def _():
        for chunk in range(CHUNKS):
            halo_copy(chunk, before).start()

    @pl.when(me == reach)
    def _():
        for j in range(reach):
            extra_copy(j).start()

    transform(reach)
    for j in range(1, share + 1):
        near_copy(j, me, near[j]).start()
    for chunk in range(CHUNKS):
        places = [(chunk * share + i, (chunk * share + i + 1) % reach) for i in range(share)]

        @pl.when(within != reach - 1)
        def _():
            halo_copy(chunk, after).wait_recv()
            for theirs, mine in places:
                stage[mine, 0] = stage[mine, 0] + halo[theirs]

        for _, mine in places:
            far_copy(mine, me, far[mine]).start()
    for j in range(share + 1, reach):
        near_copy(j, me, near[j]).start()

    recv[me] = stage[reach]
    empty = jnp.zeros(recv.shape[2:], jnp.float32)
    recv[nblocks, 1] = empty
    for i in range(1, reach):
        recv[far_base + i, 1] = empty

    @pl.when(upper_half == 1)
    def _():
        recv[0, 1] = empty

    @pl.when(upper_half == 0)
    def _():
        extra_copy(0).wait_recv()

    for j in range(reach):
        far_copy(j, far[j], far[j]).wait_recv()
    for j in range(1, reach):
        near_copy(j, near[j], near[j]).wait_recv()
    inputs[3].wait()

    combined = recv[0:nblocks, 0] + recv[1 : nblocks + 1, 1]
    spectra[...] = combined.reshape(rows, nvars * npts)

    weight = jnp.concatenate([weights_ref[v : v + 1, :] for v in range(nvars)], axis=1)
    gram_all = lax.dot_general(
        spectra[...] * weight, spectra[...], (((1,), (1,)), ((), ())),
        precision=HIGH, preferred_element_type=jnp.float32,
    )
    lane = lax.broadcasted_iota(jnp.int32, (1, rows), 1)
    sign = jnp.where(lane < half, 1.0, -1.0).astype(jnp.float32)
    group_of = lax.rem(lane, half) // nblocks
    arrival = lax.rem(lane, nblocks) * piece + 2 * group_of + jnp.where(lane < half, 0, 1)
    order[...] = lane_gather(gram_all, arrival).reshape(order.shape)
    gram = jnp.zeros((nblocks, rows), jnp.float32)
    for f in range(groups):
        upper = order[:, 2 * f, :]
        lower = order[:, 2 * f + 1, :]
        gram = jnp.where(group_of == f, upper + sign * pltpu.roll(lower, half, 1), gram)
    gram_part[side] = gram * scale

    def gram_copy(k, slot):
        peer = side_peer(k)
        return pltpu.make_async_remote_copy(
            src_ref=gram_part.at[side], dst_ref=gram_part.at[slot], send_sem=gram_send.at[k],
            recv_sem=gram_recv.at[slot], device_id={"pts": peer}, device_id_type=MESH,
        )

    for k in range(1, npart):
        gram_copy(k, side).start()
    for k in range(1, npart):
        gram_copy(k, side_peer(k)).wait_recv()
    gram = gram_part[0]
    for k in range(1, npart):
        gram = gram + gram_part[k]

    row = lax.broadcasted_iota(jnp.int32, (nblocks, rows), 0)
    trace = jnp.where((row == lax.rem(lane, nblocks)) & (lane < half), gram, 0.0)
    trace = jnp.sum(jnp.sum(trace, axis=0, keepdims=True), axis=1, keepdims=True)
    total_part[me] = jnp.broadcast_to(trace, total_part.shape[1:])

    def total_copy(k, slot):
        peer = block_peer(k)
        return pltpu.make_async_remote_copy(
            src_ref=total_part.at[me], dst_ref=total_part.at[slot], send_sem=total_send.at[k],
            recv_sem=total_recv.at[slot], device_id={"blk": peer}, device_id_type=MESH,
        )

    for k in range(1, nblocks):
        total_copy(k, me).start()

    coef, eigen = jacobi_on_lanes(gram, nblocks, groups)

    turned = -sign * half_turned(coef, half)
    for ri, block in enumerate((coef, turned)):
        for f in range(groups):
            order[:, 2 * f + ri, :] = jnp.where(group_of == f, block, 0.0)
    mixing = order[...].reshape(rows, rows).T
    modes_ref[...] = jnp.dot(
        mixing, spectra[...], precision=lax.Precision.HIGH, preferred_element_type=jnp.float32
    )

    for k in range(1, nblocks):
        total_copy(k, block_peer(k)).wait_recv()
    total = jnp.sum(total_part[...], axis=0)
    share_of = energy * eigen / total[:1]
    for f in range(groups):
        spectrum_ref[f : f + 1, :] = share_of[:, f * nblocks : (f + 1) * nblocks]
    for j in range(reach):
        far_copy(j, me, far[j]).wait_send()
    for j in range(1, reach):
        near_copy(j, me, near[j]).wait_send()

    @pl.when(within != 0)
    def _():
        for chunk in range(CHUNKS):
            halo_copy(chunk, before).wait_send()

    @pl.when(me == reach)
    def _():
        for j in range(reach):
            extra_copy(j).wait_send()

    for k in range(1, nblocks):
        total_copy(k, me).wait_send()
    for k in range(1, npart):
        gram_copy(k, side).wait_send()


def body(snapshots, weights, offsets, freqs):
    nfft, nvars, npts = snapshots.shape
    nfreq = freqs.shape[0]
    nblocks = lax.axis_size("blk")
    npart = lax.axis_size("pts")
    groups = nfreq // nblocks
    width = nvars * npts
    rows = 2 * nfreq
    scale = 1.0 / (nblocks * nvars * npts * npart)
    dma = pltpu.SemaphoreType.DMA
    vmem = pl.BlockSpec(memory_space=pltpu.VMEM)
    far_memory = pl.BlockSpec(memory_space=pltpu.HBM)
    modes, spectrum = pl.pallas_call(
        functools.partial(pipeline_kernel, nblocks, npart, groups, scale, float(nfreq * nblocks)),
        out_shape=(
            jax.ShapeDtypeStruct((rows, width), jnp.float32),
            jax.ShapeDtypeStruct((groups, nblocks), jnp.float32),
        ),
        in_specs=[far_memory] * 4,
        out_specs=(vmem, vmem),
        scratch_shapes=[
            pltpu.VMEM((nvars, nfft, npts), jnp.float32),
            pltpu.VMEM((nvars, npts), jnp.float32),
            pltpu.SMEM((nblocks,), jnp.int32),
            pltpu.SMEM((nfreq,), jnp.int32),
            pltpu.VMEM((2 * rows, nfft), jnp.float32),
            pltpu.VMEM((nblocks, 2, 2 * groups, width), jnp.float32),
            pltpu.VMEM((nblocks + 1, 2, 2 * groups, width), jnp.float32),
            pltpu.VMEM((nblocks // 2, 2 * groups, width), jnp.float32),
            pltpu.VMEM((rows, width), jnp.float32),
            pltpu.VMEM((nblocks, 2 * groups, rows), jnp.float32),
            pltpu.VMEM((npart, nblocks, rows), jnp.float32),
            pltpu.VMEM((nblocks, 8, rows), jnp.float32),
            dma((4,)),
            dma((nblocks,)), dma((nblocks,)),
            dma((CHUNKS,)), dma((CHUNKS,)),
            dma((nblocks // 2,)), dma((1,)),
            dma((npart,)), dma((npart,)),
            dma((nblocks,)), dma((nblocks,)),
        ],
        compiler_params=pltpu.CompilerParams(
            collective_id=0, has_side_effects=True, vmem_limit_bytes=60 * 1024 * 1024
        ),
    )(snapshots.transpose(1, 0, 2), weights, offsets, freqs)
    modes = modes.reshape(2, groups, nblocks, nvars, npts).transpose(1, 2, 0, 3, 4)
    return modes, spectrum


def solution(mesh):
    return jax.shard_map(
        body,
        mesh=mesh,
        in_specs=(P("blk", None, "pts"), P(None, "pts"), P(), P()),
        out_specs=(P("blk", None, None, None, "pts"), P("blk", None)),
        check_vma=False,
    )
```

```python
import functools
import math

import jax
import jax.numpy as jnp
from jax import lax
from jax.experimental import pallas as pl
from jax.experimental.pallas import tpu as pltpu
from jax.sharding import PartitionSpec as P

SWEEPS = 2


HIGH = lax.Precision.HIGHEST
DAMPING = 0.01
CHUNKS = 2
MESH = pl.DeviceIdType.MESH


def half_turned(row, half):
    return pltpu.roll(row, half, 1)


def lane_gather(block, index):
    rows = max(block.shape[0], 8)
    wide = jnp.broadcast_to(block, (rows, block.shape[1]))
    index = index if index.shape == wide.shape else jnp.broadcast_to(index[:1], wide.shape)
    return jnp.take_along_axis(wide, index, axis=1, mode="promise_in_bounds")[: block.shape[0]]


def jacobi_on_lanes(gram, count, groups):
    half = groups * count
    lanes = 2 * half
    lane = lax.broadcasted_iota(jnp.int32, (8, lanes), 1)
    column = lax.rem(lane, count)
    first = lane - column
    in_real = lane[:1] < half
    row = lax.broadcasted_iota(jnp.int32, (count, lanes), 0)
    eye = jnp.where(row == column[:1], 1.0, 0.0).astype(jnp.float32)
    turned = half_turned(gram, half)
    prod_r = jnp.where(in_real, gram, turned)
    prod_i = jnp.where(in_real, turned, gram)
    diag = jnp.sum(prod_r * eye, axis=0, keepdims=True)

    def partner_of(turn):
        mirror = 2 * turn - column
        mirror = jnp.where(mirror < 0, mirror + (count - 1), mirror)
        mirror = jnp.where(mirror >= count - 1, mirror - (count - 1), mirror)
        return jnp.where(column == count - 1, turn, jnp.where(column == turn, count - 1, mirror))

    def advance(counter, carry):
        vec_r, vec_i, prod_r, prod_i, diag, partner = carry
        following = partner_of(lax.rem(counter + 1, count - 1))
        parity = jnp.where(column < partner, 1.0, -1.0).astype(jnp.float32)[:1]
        same = first + partner
        prod_sr = lane_gather(prod_r, same)
        prod_si = lane_gather(prod_i, same)
        diag_pair = lane_gather(diag, same)
        vec_sr = lane_gather(vec_r, same)
        vec_si = lane_gather(vec_i, same)
        pair_real = jnp.sum(vec_r * prod_sr + vec_i * prod_si, axis=0, keepdims=True)
        pair_imag = jnp.sum(vec_r * prod_si - vec_i * prod_sr, axis=0, keepdims=True)
        delta = parity * (diag_pair - diag)
        size4 = 4.0 * (pair_real * pair_real + pair_imag * pair_imag)
        radius = jnp.sqrt(delta * delta + size4)
        upper = radius + (delta + DAMPING * (diag + diag_pair))
        inverse = lax.rsqrt(upper * upper + size4)
        cosine = upper * inverse
        scale = 2.0 * parity * inverse
        coef_r = -scale * pair_real
        coef_i = scale * pair_imag
        sine_sq = size4 * inverse * inverse
        diag = cosine * cosine * diag + sine_sq * diag_pair - parity * cosine * size4 * inverse

        def turn_pair(real, imag, swap_real, swap_imag):
            return (
                real * cosine + (swap_real * coef_r - swap_imag * coef_i),
                imag * cosine + (swap_real * coef_i + swap_imag * coef_r),
            )

        prod_r, prod_i = turn_pair(prod_r, prod_i, prod_sr, prod_si)
        vec_r, vec_i = turn_pair(vec_r, vec_i, vec_sr, vec_si)
        return vec_r, vec_i, prod_r, prod_i, diag, following

    state = (eye, jnp.zeros_like(eye), prod_r, prod_i, diag, partner_of(0))
    state = lax.fori_loop(0, SWEEPS * (count - 1), advance, state, unroll=3)
    vec_r, vec_i, _, _, eigen, _ = state
    sum_r = jnp.sum(vec_r, axis=0, keepdims=True)
    sum_i = jnp.sum(vec_i, axis=0, keepdims=True)
    magnitude = jnp.sqrt(sum_r * sum_r + sum_i * sum_i)
    scaling = 1.0 / (jnp.maximum(magnitude, 1.0) * jnp.sqrt(count * (eigen + 1e-06)))
    phase_r = sum_r * scaling
    phase_i = -sum_i * scaling
    coef = jnp.where(
        in_real, vec_r * phase_r - vec_i * phase_i, vec_r * phase_i + vec_i * phase_r
    )
    return coef, eigen


def signed_wave(base, index):
    lanes = base.shape[1]
    value = lane_gather(base, jnp.bitwise_and(index, lanes - 1))
    return jnp.where(jnp.bitwise_and(index, lanes) == 0, value, -value)


def write_table(table_ref, offsets_ref, freqs_ref, me, groups, owners):
    rows, nfft = table_ref.shape
    half = nfft // 2
    lane = lax.broadcasted_iota(jnp.int32, (8, half), 1)
    sub = lax.broadcasted_iota(jnp.int32, (8, half), 0)
    base = jnp.cos(2.0 * math.pi / nfft * lane.astype(jnp.float32))
    own = offsets_ref[me]
    before = jnp.where(me > 0, offsets_ref[jnp.maximum(me - 1, 0)], 0)
    quarter = jnp.where(lax.rem(sub, 2) == 1, nfft // 4, 0)
    windows = {}
    for tile in range(rows // 8):
        tile_rows = range(8 * tile, 8 * tile + 8)
        pieces = tuple(r % (4 * groups) // (2 * groups) for r in tile_rows)
        freq = [owners[r // (4 * groups)] * groups + r % (2 * groups) // 2 for r in tile_rows]
        freq_rows = jnp.full((8, half), freqs_ref[freq[0]], jnp.int32)
        for s in range(2, 8, 2):
            freq_rows = jnp.where(sub >= s, freqs_ref[freq[s]], freq_rows)
        if pieces not in windows:
            tail = jnp.zeros((8, half), jnp.bool_)
            for s in range(8):
                if pieces[s]:
                    tail = tail | (sub == s)
            start = jnp.where(tail, before, own)
            window = []
            for h in range(2):
                lag = lane + h * half - start
                hann = 0.5 - 0.5 * signed_wave(base, lag)
                valid = (tail & (lag < 0)) | (jnp.logical_not(tail) & (lag >= 0))
                window.append((lag, jnp.where(valid, hann, 0.0) / math.sqrt(nfft)))
            windows[pieces] = window
        for h in range(2):
            lag, factor = windows[pieces][h]
            wave = signed_wave(base, freq_rows * lag + quarter)
            table_ref[8 * tile : 8 * tile + 8, h * half : (h + 1) * half] = factor * wave


def pipeline_kernel(
    nblocks, npart, groups, scale, energy,
    snaps_hbm, weights_hbm, offsets_hbm, freqs_hbm, modes_ref, spectrum_ref,
    snaps_ref, weights_ref, offsets_ref, freqs_ref,
    table, stage, recv, halo, spectra, order, gram_part, total_part,
    input_sem, send_sem, recv_sem, halo_send, halo_recv, extra_send, extra_recv,
    gram_send, gram_recv, total_send, total_recv,
):
    inputs = [
        pltpu.make_async_copy(src, dst, input_sem.at[i])
        for i, (src, dst) in enumerate((
            (offsets_hbm, offsets_ref), (freqs_hbm, freqs_ref),
            (snaps_hbm, snaps_ref), (weights_hbm, weights_ref),
        ))
    ]
    for copy in inputs:
        copy.start()
    me = lax.axis_index("blk")
    side = lax.axis_index("pts")
    nvars, nfft, npts = snaps_ref.shape
    rows = 2 * groups * nblocks
    half = rows // 2
    piece = 2 * groups
    reach = nblocks // 2
    upper_half = me // reach
    within = lax.rem(me, reach)
    far_base = (1 - upper_half) * reach
    near_base = upper_half * reach
    far = [far_base + lax.rem(within + j, reach) for j in range(reach)]
    near = [near_base + lax.rem(within + j, reach) for j in range(reach)]
    owners = far + near

    def block_peer(k):
        return lax.rem(me + k, nblocks)

    def side_peer(k):
        return lax.rem(side + k, npart)

    barrier = pltpu.get_barrier_semaphore()
    for k in range(1, nblocks):
        pl.semaphore_signal(barrier, inc=1, device_id={"blk": block_peer(k)}, device_id_type=MESH)
    for k in range(1, npart):
        pl.semaphore_signal(barrier, inc=1, device_id={"pts": side_peer(k)}, device_id_type=MESH)

    inputs[0].wait()
    inputs[1].wait()
    write_table(table, offsets_ref, freqs_ref, me, groups, owners)
    inputs[2].wait()
    snaps = jnp.concatenate([snaps_ref[v] for v in range(nvars)], axis=1)

    def transform(first):
        part = jnp.dot(
            table[2 * piece * first : 2 * piece * (first + reach), :], snaps,
            precision=lax.Precision.HIGH, preferred_element_type=jnp.float32,
        )
        for j in range(reach):
            at = 2 * piece * j
            stage[first + j, 0] = part[at : at + piece]
            stage[first + j, 1] = part[at + piece : at + 2 * piece]

    def remote(src, dst, sent, received, peer):
        return pltpu.make_async_remote_copy(
            src_ref=src, dst_ref=dst, send_sem=sent, recv_sem=received,
            device_id={"blk": peer}, device_id_type=MESH,
        )

    share = reach // CHUNKS
    before = jnp.maximum(me - 1, 0)
    after = jnp.minimum(me + 1, nblocks - 1)

    def halo_copy(chunk, peer):
        places = pl.ds(chunk * share, share)
        return remote(
            stage.at[places, 1], halo.at[places], halo_send.at[chunk], halo_recv.at[chunk], peer
        )

    def far_copy(j, slot, peer):
        return remote(stage.at[j, 0], recv.at[slot, 0], send_sem.at[j], recv_sem.at[slot], peer)

    def near_copy(j, slot, peer):
        at = reach + j
        return remote(stage.at[at], recv.at[slot], send_sem.at[at], recv_sem.at[slot], peer)

    def extra_copy(j):
        return remote(stage.at[j, 1], recv.at[reach, 1], extra_send.at[j], extra_recv.at[0], far[j])

    transform(0)
    pl.semaphore_wait(barrier, nblocks - 1 + npart - 1)

    @pl.when(within != 0)
    def _():
        for chunk in range(CHUNKS):
            halo_copy(chunk, before).start()

    @pl.when(me == reach)
    def _():
        for j in range(reach):
            extra_copy(j).start()

    transform(reach)
    for j in range(1, share + 1):
        near_copy(j, me, near[j]).start()
    for chunk in range(CHUNKS):
        places = [(chunk * share + i, (chunk * share + i + 1) % reach) for i in range(share)]

        @pl.when(within != reach - 1)
        def _():
            halo_copy(chunk, after).wait_recv()
            for theirs, mine in places:
                stage[mine, 0] = stage[mine, 0] + halo[theirs]

        for _, mine in places:
            far_copy(mine, me, far[mine]).start()
    for j in range(share + 1, reach):
        near_copy(j, me, near[j]).start()

    recv[me] = stage[reach]
    empty = jnp.zeros(recv.shape[2:], jnp.float32)
    recv[nblocks, 1] = empty
    for i in range(1, reach):
        recv[far_base + i, 1] = empty

    @pl.when(upper_half == 1)
    def _():
        recv[0, 1] = empty

    @pl.when(upper_half == 0)
    def _():
        extra_copy(0).wait_recv()

    for j in range(reach):
        far_copy(j, far[j], far[j]).wait_recv()
    for j in range(1, reach):
        near_copy(j, near[j], near[j]).wait_recv()
    inputs[3].wait()

    combined = recv[0:nblocks, 0] + recv[1 : nblocks + 1, 1]
    spectra[...] = combined.reshape(rows, nvars * npts)

    weight = jnp.concatenate([weights_ref[v : v + 1, :] for v in range(nvars)], axis=1)
    gram_all = lax.dot_general(
        spectra[...] * weight, spectra[...], (((1,), (1,)), ((), ())),
        precision=HIGH, preferred_element_type=jnp.float32,
    )
    lane = lax.broadcasted_iota(jnp.int32, (1, rows), 1)
    sign = jnp.where(lane < half, 1.0, -1.0).astype(jnp.float32)
    group_of = lax.rem(lane, half) // nblocks
    arrival = lax.rem(lane, nblocks) * piece + 2 * group_of + jnp.where(lane < half, 0, 1)
    order[...] = lane_gather(gram_all, arrival).reshape(order.shape)
    gram = jnp.zeros((nblocks, rows), jnp.float32)
    for f in range(groups):
        upper = order[:, 2 * f, :]
        lower = order[:, 2 * f + 1, :]
        gram = jnp.where(group_of == f, upper + sign * pltpu.roll(lower, half, 1), gram)
    gram_part[side] = gram * scale

    def gram_copy(k, slot):
        peer = side_peer(k)
        return pltpu.make_async_remote_copy(
            src_ref=gram_part.at[side], dst_ref=gram_part.at[slot], send_sem=gram_send.at[k],
            recv_sem=gram_recv.at[slot], device_id={"pts": peer}, device_id_type=MESH,
        )

    for k in range(1, npart):
        gram_copy(k, side).start()
    for k in range(1, npart):
        gram_copy(k, side_peer(k)).wait_recv()
    gram = gram_part[0]
    for k in range(1, npart):
        gram = gram + gram_part[k]

    row = lax.broadcasted_iota(jnp.int32, (nblocks, rows), 0)
    trace = jnp.where((row == lax.rem(lane, nblocks)) & (lane < half), gram, 0.0)
    trace = jnp.sum(jnp.sum(trace, axis=0, keepdims=True), axis=1, keepdims=True)
    total_part[me] = jnp.broadcast_to(trace, total_part.shape[1:])

    def total_copy(k, slot):
        peer = block_peer(k)
        return pltpu.make_async_remote_copy(
            src_ref=total_part.at[me], dst_ref=total_part.at[slot], send_sem=total_send.at[k],
            recv_sem=total_recv.at[slot], device_id={"blk": peer}, device_id_type=MESH,
        )

    for k in range(1, nblocks):
        total_copy(k, me).start()

    coef, eigen = jacobi_on_lanes(gram, nblocks, groups)

    turned = -sign * half_turned(coef, half)
    for ri, block in enumerate((coef, turned)):
        for f in range(groups):
            order[:, 2 * f + ri, :] = jnp.where(group_of == f, block, 0.0)
    mixing = order[...].reshape(rows, rows).T
    modes = jnp.dot(
        mixing, spectra[...], precision=lax.Precision.HIGH, preferred_element_type=jnp.float32
    )
    for v in range(nvars):
        for ri in range(2):
            modes_ref[pl.ds(2 * v + ri, half, stride=2 * nvars), :] = modes[
                ri * half : (ri + 1) * half, v * npts : (v + 1) * npts
            ]

    for k in range(1, nblocks):
        total_copy(k, block_peer(k)).wait_recv()
    total = jnp.sum(total_part[...], axis=0)
    share_of = energy * eigen / total[:1]
    for f in range(groups):
        spectrum_ref[f : f + 1, :] = share_of[:, f * nblocks : (f + 1) * nblocks]
    for j in range(reach):
        far_copy(j, me, far[j]).wait_send()
    for j in range(1, reach):
        near_copy(j, me, near[j]).wait_send()

    @pl.when(within != 0)
    def _():
        for chunk in range(CHUNKS):
            halo_copy(chunk, before).wait_send()

    @pl.when(me == reach)
    def _():
        for j in range(reach):
            extra_copy(j).wait_send()

    for k in range(1, nblocks):
        total_copy(k, me).wait_send()
    for k in range(1, npart):
        gram_copy(k, side).wait_send()


def body(snapshots, weights, offsets, freqs):
    nfft, nvars, npts = snapshots.shape
    nfreq = freqs.shape[0]
    nblocks = lax.axis_size("blk")
    npart = lax.axis_size("pts")
    groups = nfreq // nblocks
    width = nvars * npts
    rows = 2 * nfreq
    scale = 1.0 / (nblocks * nvars * npts * npart)
    dma = pltpu.SemaphoreType.DMA
    vmem = pl.BlockSpec(memory_space=pltpu.VMEM)
    far_memory = pl.BlockSpec(memory_space=pltpu.HBM)
    modes, spectrum = pl.pallas_call(
        functools.partial(pipeline_kernel, nblocks, npart, groups, scale, float(nfreq * nblocks)),
        out_shape=(
            jax.ShapeDtypeStruct((rows * nvars, npts), jnp.float32),
            jax.ShapeDtypeStruct((groups, nblocks), jnp.float32),
        ),
        in_specs=[far_memory] * 4,
        out_specs=(vmem, vmem),
        scratch_shapes=[
            pltpu.VMEM((nvars, nfft, npts), jnp.float32),
            pltpu.VMEM((nvars, npts), jnp.float32),
            pltpu.SMEM((nblocks,), jnp.int32),
            pltpu.SMEM((nfreq,), jnp.int32),
            pltpu.VMEM((2 * rows, nfft), jnp.float32),
            pltpu.VMEM((nblocks, 2, 2 * groups, width), jnp.float32),
            pltpu.VMEM((nblocks + 1, 2, 2 * groups, width), jnp.float32),
            pltpu.VMEM((nblocks // 2, 2 * groups, width), jnp.float32),
            pltpu.VMEM((rows, width), jnp.float32),
            pltpu.VMEM((nblocks, 2 * groups, rows), jnp.float32),
            pltpu.VMEM((npart, nblocks, rows), jnp.float32),
            pltpu.VMEM((nblocks, 8, rows), jnp.float32),
            dma((4,)),
            dma((nblocks,)), dma((nblocks,)),
            dma((CHUNKS,)), dma((CHUNKS,)),
            dma((nblocks // 2,)), dma((1,)),
            dma((npart,)), dma((npart,)),
            dma((nblocks,)), dma((nblocks,)),
        ],
        compiler_params=pltpu.CompilerParams(
            collective_id=0, has_side_effects=True, vmem_limit_bytes=60 * 1024 * 1024
        ),
    )(snapshots.transpose(1, 0, 2), weights, offsets, freqs)
    modes = modes.reshape(groups, nblocks, nvars, 2, npts).transpose(0, 1, 3, 2, 4)
    return modes, spectrum


def solution(mesh):
    return jax.shard_map(
        body,
        mesh=mesh,
        in_specs=(P("blk", None, "pts"), P(None, "pts"), P(), P()),
        out_specs=(P("blk", None, None, None, "pts"), P("blk", None)),
        check_vma=False,
    )
```

```python
import functools
import math

import jax
import jax.numpy as jnp
from jax import lax
from jax.experimental import pallas as pl
from jax.experimental.pallas import tpu as pltpu
from jax.sharding import PartitionSpec as P

SWEEPS = 2


HIGH = lax.Precision.HIGHEST
DAMPING = 0.01
CHUNKS = 2
MESH = pl.DeviceIdType.MESH


def half_turned(row, half):
    return pltpu.roll(row, half, 1)


def lane_gather(block, index):
    rows = max(block.shape[0], 8)
    wide = jnp.broadcast_to(block, (rows, block.shape[1]))
    index = index if index.shape == wide.shape else jnp.broadcast_to(index[:1], wide.shape)
    return jnp.take_along_axis(wide, index, axis=1, mode="promise_in_bounds")[: block.shape[0]]


def jacobi_on_lanes(gram, count, groups):
    half = groups * count
    lanes = 2 * half
    lane = lax.broadcasted_iota(jnp.int32, (8, lanes), 1)
    column = lax.rem(lane, count)
    first = lane - column
    in_real = lane[:1] < half
    row = lax.broadcasted_iota(jnp.int32, (count, lanes), 0)
    eye = jnp.where(row == column[:1], 1.0, 0.0).astype(jnp.float32)
    turned = half_turned(gram, half)
    prod_r = jnp.where(in_real, gram, turned)
    prod_i = jnp.where(in_real, turned, gram)
    diag = jnp.sum(prod_r * eye, axis=0, keepdims=True)

    def partner_of(turn):
        mirror = 2 * turn - column
        mirror = jnp.where(mirror < 0, mirror + (count - 1), mirror)
        mirror = jnp.where(mirror >= count - 1, mirror - (count - 1), mirror)
        return jnp.where(column == count - 1, turn, jnp.where(column == turn, count - 1, mirror))

    def advance(counter, carry):
        vec_r, vec_i, prod_r, prod_i, diag, partner = carry
        following = partner_of(lax.rem(counter + 1, count - 1))
        parity = jnp.where(column < partner, 1.0, -1.0).astype(jnp.float32)[:1]
        same = first + partner
        prod_sr = lane_gather(prod_r, same)
        prod_si = lane_gather(prod_i, same)
        diag_pair = lane_gather(diag, same)
        vec_sr = lane_gather(vec_r, same)
        vec_si = lane_gather(vec_i, same)
        pair_real = jnp.sum(vec_r * prod_sr + vec_i * prod_si, axis=0, keepdims=True)
        pair_imag = jnp.sum(vec_r * prod_si - vec_i * prod_sr, axis=0, keepdims=True)
        delta = parity * (diag_pair - diag)
        size4 = 4.0 * (pair_real * pair_real + pair_imag * pair_imag)
        radius = jnp.sqrt(delta * delta + size4)
        upper = radius + (delta + DAMPING * (diag + diag_pair))
        inverse = lax.rsqrt(upper * upper + size4)
        cosine = upper * inverse
        scale = 2.0 * parity * inverse
        coef_r = -scale * pair_real
        coef_i = scale * pair_imag
        sine_sq = size4 * inverse * inverse
        diag = cosine * cosine * diag + sine_sq * diag_pair - parity * cosine * size4 * inverse

        def turn_pair(real, imag, swap_real, swap_imag):
            return (
                real * cosine + (swap_real * coef_r - swap_imag * coef_i),
                imag * cosine + (swap_real * coef_i + swap_imag * coef_r),
            )

        prod_r, prod_i = turn_pair(prod_r, prod_i, prod_sr, prod_si)
        vec_r, vec_i = turn_pair(vec_r, vec_i, vec_sr, vec_si)
        return vec_r, vec_i, prod_r, prod_i, diag, following

    state = (eye, jnp.zeros_like(eye), prod_r, prod_i, diag, partner_of(0))
    state = lax.fori_loop(0, SWEEPS * (count - 1), advance, state, unroll=3)
    vec_r, vec_i, _, _, eigen, _ = state
    sum_r = jnp.sum(vec_r, axis=0, keepdims=True)
    sum_i = jnp.sum(vec_i, axis=0, keepdims=True)
    magnitude = jnp.sqrt(sum_r * sum_r + sum_i * sum_i)
    scaling = 1.0 / (jnp.maximum(magnitude, 1.0) * jnp.sqrt(count * (eigen + 1e-06)))
    phase_r = sum_r * scaling
    phase_i = -sum_i * scaling
    coef = jnp.where(
        in_real, vec_r * phase_r - vec_i * phase_i, vec_r * phase_i + vec_i * phase_r
    )
    return coef, eigen


def signed_wave(base, index):
    lanes = base.shape[1]
    value = lane_gather(base, jnp.bitwise_and(index, lanes - 1))
    return jnp.where(jnp.bitwise_and(index, lanes) == 0, value, -value)


def write_table(table_ref, offsets_ref, freqs_ref, me, groups, owners):
    rows, nfft = table_ref.shape
    half = nfft // 2
    lane = lax.broadcasted_iota(jnp.int32, (8, half), 1)
    sub = lax.broadcasted_iota(jnp.int32, (8, half), 0)
    base = jnp.cos(2.0 * math.pi / nfft * lane.astype(jnp.float32))
    own = offsets_ref[me]
    before = jnp.where(me > 0, offsets_ref[jnp.maximum(me - 1, 0)], 0)
    quarter = jnp.where(lax.rem(sub, 2) == 1, nfft // 4, 0)
    windows = {}
    for tile in range(rows // 8):
        tile_rows = range(8 * tile, 8 * tile + 8)
        pieces = tuple(r % (4 * groups) // (2 * groups) for r in tile_rows)
        freq = [owners[r // (4 * groups)] * groups + r % (2 * groups) // 2 for r in tile_rows]
        freq_rows = jnp.full((8, half), freqs_ref[freq[0]], jnp.int32)
        for s in range(2, 8, 2):
            freq_rows = jnp.where(sub >= s, freqs_ref[freq[s]], freq_rows)
        if pieces not in windows:
            tail = jnp.zeros((8, half), jnp.bool_)
            for s in range(8):
                if pieces[s]:
                    tail = tail | (sub == s)
            start = jnp.where(tail, before, own)
            window = []
            for h in range(2):
                lag = lane + h * half - start
                hann = 0.5 - 0.5 * signed_wave(base, lag)
                valid = (tail & (lag < 0)) | (jnp.logical_not(tail) & (lag >= 0))
                window.append((lag, jnp.where(valid, hann, 0.0) / math.sqrt(nfft)))
            windows[pieces] = window
        for h in range(2):
            lag, factor = windows[pieces][h]
            wave = signed_wave(base, freq_rows * lag + quarter)
            table_ref[8 * tile : 8 * tile + 8, h * half : (h + 1) * half] = factor * wave


def pipeline_kernel(
    nblocks, npart, groups, scale, energy,
    snaps_hbm, weights_hbm, offsets_hbm, freqs_hbm, spectra_hbm, mixing_ref, spectrum_ref,
    snaps_ref, weights_ref, offsets_ref, freqs_ref,
    table, stage, recv, halo, spectra, order, gram_part, total_part,
    input_sem, output_sem, send_sem, recv_sem, halo_send, halo_recv, extra_send, extra_recv,
    gram_send, gram_recv, total_send, total_recv,
):
    inputs = [
        pltpu.make_async_copy(src, dst, input_sem.at[i])
        for i, (src, dst) in enumerate((
            (offsets_hbm, offsets_ref), (freqs_hbm, freqs_ref),
            (snaps_hbm, snaps_ref), (weights_hbm, weights_ref),
        ))
    ]
    for copy in inputs:
        copy.start()
    me = lax.axis_index("blk")
    side = lax.axis_index("pts")
    nvars, nfft, npts = snaps_ref.shape
    rows = 2 * groups * nblocks
    half = rows // 2
    piece = 2 * groups
    reach = nblocks // 2
    upper_half = me // reach
    within = lax.rem(me, reach)
    far_base = (1 - upper_half) * reach
    near_base = upper_half * reach
    far = [far_base + lax.rem(within + j, reach) for j in range(reach)]
    near = [near_base + lax.rem(within + j, reach) for j in range(reach)]
    owners = far + near

    def block_peer(k):
        return lax.rem(me + k, nblocks)

    def side_peer(k):
        return lax.rem(side + k, npart)

    barrier = pltpu.get_barrier_semaphore()
    for k in range(1, nblocks):
        pl.semaphore_signal(barrier, inc=1, device_id={"blk": block_peer(k)}, device_id_type=MESH)
    for k in range(1, npart):
        pl.semaphore_signal(barrier, inc=1, device_id={"pts": side_peer(k)}, device_id_type=MESH)

    inputs[0].wait()
    inputs[1].wait()
    write_table(table, offsets_ref, freqs_ref, me, groups, owners)
    inputs[2].wait()
    snaps = jnp.concatenate([snaps_ref[v] for v in range(nvars)], axis=1)

    def transform(first):
        part = jnp.dot(
            table[2 * piece * first : 2 * piece * (first + reach), :], snaps,
            precision=lax.Precision.HIGH, preferred_element_type=jnp.float32,
        )
        for j in range(reach):
            at = 2 * piece * j
            stage[first + j, 0] = part[at : at + piece]
            stage[first + j, 1] = part[at + piece : at + 2 * piece]

    def remote(src, dst, sent, received, peer):
        return pltpu.make_async_remote_copy(
            src_ref=src, dst_ref=dst, send_sem=sent, recv_sem=received,
            device_id={"blk": peer}, device_id_type=MESH,
        )

    share = reach // CHUNKS
    before = jnp.maximum(me - 1, 0)
    after = jnp.minimum(me + 1, nblocks - 1)

    def halo_copy(chunk, peer):
        places = pl.ds(chunk * share, share)
        return remote(
            stage.at[places, 1], halo.at[places], halo_send.at[chunk], halo_recv.at[chunk], peer
        )

    def far_copy(j, slot, peer):
        return remote(stage.at[j, 0], recv.at[slot, 0], send_sem.at[j], recv_sem.at[slot], peer)

    def near_copy(j, slot, peer):
        at = reach + j
        return remote(stage.at[at], recv.at[slot], send_sem.at[at], recv_sem.at[slot], peer)

    def extra_copy(j):
        return remote(stage.at[j, 1], recv.at[reach, 1], extra_send.at[j], extra_recv.at[0], far[j])

    transform(0)
    pl.semaphore_wait(barrier, nblocks - 1 + npart - 1)

    @pl.when(within != 0)
    def _():
        for chunk in range(CHUNKS):
            halo_copy(chunk, before).start()

    @pl.when(me == reach)
    def _():
        for j in range(reach):
            extra_copy(j).start()

    transform(reach)
    for j in range(1, share + 1):
        near_copy(j, me, near[j]).start()
    for chunk in range(CHUNKS):
        places = [(chunk * share + i, (chunk * share + i + 1) % reach) for i in range(share)]

        @pl.when(within != reach - 1)
        def _():
            halo_copy(chunk, after).wait_recv()
            for theirs, mine in places:
                stage[mine, 0] = stage[mine, 0] + halo[theirs]

        for _, mine in places:
            far_copy(mine, me, far[mine]).start()
    for j in range(share + 1, reach):
        near_copy(j, me, near[j]).start()

    recv[me] = stage[reach]
    empty = jnp.zeros(recv.shape[2:], jnp.float32)
    recv[nblocks, 1] = empty
    for i in range(1, reach):
        recv[far_base + i, 1] = empty

    @pl.when(upper_half == 1)
    def _():
        recv[0, 1] = empty

    @pl.when(upper_half == 0)
    def _():
        extra_copy(0).wait_recv()

    for j in range(reach):
        far_copy(j, far[j], far[j]).wait_recv()
    for j in range(1, reach):
        near_copy(j, near[j], near[j]).wait_recv()
    inputs[3].wait()

    combined = recv[0:nblocks, 0] + recv[1 : nblocks + 1, 1]
    spectra[...] = combined.reshape(rows, nvars * npts)
    spectra_out = pltpu.make_async_copy(spectra, spectra_hbm, output_sem.at[0])
    spectra_out.start()

    weight = jnp.concatenate([weights_ref[v : v + 1, :] for v in range(nvars)], axis=1)
    gram_all = lax.dot_general(
        spectra[...] * weight, spectra[...], (((1,), (1,)), ((), ())),
        precision=HIGH, preferred_element_type=jnp.float32,
    )
    lane = lax.broadcasted_iota(jnp.int32, (1, rows), 1)
    sign = jnp.where(lane < half, 1.0, -1.0).astype(jnp.float32)
    group_of = lax.rem(lane, half) // nblocks
    arrival = lax.rem(lane, nblocks) * piece + 2 * group_of + jnp.where(lane < half, 0, 1)
    order[...] = lane_gather(gram_all, arrival).reshape(order.shape)
    gram = jnp.zeros((nblocks, rows), jnp.float32)
    for f in range(groups):
        upper = order[:, 2 * f, :]
        lower = order[:, 2 * f + 1, :]
        gram = jnp.where(group_of == f, upper + sign * pltpu.roll(lower, half, 1), gram)
    gram_part[side] = gram * scale

    def gram_copy(k, slot):
        peer = side_peer(k)
        return pltpu.make_async_remote_copy(
            src_ref=gram_part.at[side], dst_ref=gram_part.at[slot], send_sem=gram_send.at[k],
            recv_sem=gram_recv.at[slot], device_id={"pts": peer}, device_id_type=MESH,
        )

    for k in range(1, npart):
        gram_copy(k, side).start()
    for k in range(1, npart):
        gram_copy(k, side_peer(k)).wait_recv()
    gram = gram_part[0]
    for k in range(1, npart):
        gram = gram + gram_part[k]

    row = lax.broadcasted_iota(jnp.int32, (nblocks, rows), 0)
    trace = jnp.where((row == lax.rem(lane, nblocks)) & (lane < half), gram, 0.0)
    trace = jnp.sum(jnp.sum(trace, axis=0, keepdims=True), axis=1, keepdims=True)
    total_part[me] = jnp.broadcast_to(trace, total_part.shape[1:])

    def total_copy(k, slot):
        peer = block_peer(k)
        return pltpu.make_async_remote_copy(
            src_ref=total_part.at[me], dst_ref=total_part.at[slot], send_sem=total_send.at[k],
            recv_sem=total_recv.at[slot], device_id={"blk": peer}, device_id_type=MESH,
        )

    for k in range(1, nblocks):
        total_copy(k, me).start()

    coef, eigen = jacobi_on_lanes(gram, nblocks, groups)

    turned = -sign * half_turned(coef, half)
    for ri, block in enumerate((coef, turned)):
        for f in range(groups):
            order[:, 2 * f + ri, :] = jnp.where(group_of == f, block, 0.0)
    mixing_ref[...] = order[...].reshape(rows, rows).T

    for k in range(1, nblocks):
        total_copy(k, block_peer(k)).wait_recv()
    total = jnp.sum(total_part[...], axis=0)
    share_of = energy * eigen / total[:1]
    for f in range(groups):
        spectrum_ref[f : f + 1, :] = share_of[:, f * nblocks : (f + 1) * nblocks]
    spectra_out.wait()
    for j in range(reach):
        far_copy(j, me, far[j]).wait_send()
    for j in range(1, reach):
        near_copy(j, me, near[j]).wait_send()

    @pl.when(within != 0)
    def _():
        for chunk in range(CHUNKS):
            halo_copy(chunk, before).wait_send()

    @pl.when(me == reach)
    def _():
        for j in range(reach):
            extra_copy(j).wait_send()

    for k in range(1, nblocks):
        total_copy(k, me).wait_send()
    for k in range(1, npart):
        gram_copy(k, side).wait_send()


def modes_kernel(nvars, spectra_ref, mixing_ref, share_ref, modes_ref, spectrum_ref):
    rows, width = spectra_ref.shape
    half = rows // 2
    npts = width // nvars
    spectrum_ref[...] = share_ref[...]
    modes = jnp.dot(
        mixing_ref[...], spectra_ref[...], precision=lax.Precision.HIGH,
        preferred_element_type=jnp.float32,
    )
    for v in range(nvars):
        for ri in range(2):
            modes_ref[pl.ds(2 * v + ri, half, stride=2 * nvars), :] = modes[
                ri * half : (ri + 1) * half, v * npts : (v + 1) * npts
            ]


def body(snapshots, weights, offsets, freqs):
    nfft, nvars, npts = snapshots.shape
    nfreq = freqs.shape[0]
    nblocks = lax.axis_size("blk")
    npart = lax.axis_size("pts")
    groups = nfreq // nblocks
    width = nvars * npts
    rows = 2 * nfreq
    scale = 1.0 / (nblocks * nvars * npts * npart)
    dma = pltpu.SemaphoreType.DMA
    vmem = pl.BlockSpec(memory_space=pltpu.VMEM)
    far_memory = pl.BlockSpec(memory_space=pltpu.HBM)
    spectra, mixing, share = pl.pallas_call(
        functools.partial(pipeline_kernel, nblocks, npart, groups, scale, float(nfreq * nblocks)),
        out_shape=(
            jax.ShapeDtypeStruct((rows, width), jnp.float32),
            jax.ShapeDtypeStruct((rows, rows), jnp.float32),
            jax.ShapeDtypeStruct((groups, nblocks), jnp.float32),
        ),
        in_specs=[far_memory] * 4,
        out_specs=(far_memory, vmem, vmem),
        scratch_shapes=[
            pltpu.VMEM((nvars, nfft, npts), jnp.float32),
            pltpu.VMEM((nvars, npts), jnp.float32),
            pltpu.SMEM((nblocks,), jnp.int32),
            pltpu.SMEM((nfreq,), jnp.int32),
            pltpu.VMEM((2 * rows, nfft), jnp.float32),
            pltpu.VMEM((nblocks, 2, 2 * groups, width), jnp.float32),
            pltpu.VMEM((nblocks + 1, 2, 2 * groups, width), jnp.float32),
            pltpu.VMEM((nblocks // 2, 2 * groups, width), jnp.float32),
            pltpu.VMEM((rows, width), jnp.float32),
            pltpu.VMEM((nblocks, 2 * groups, rows), jnp.float32),
            pltpu.VMEM((npart, nblocks, rows), jnp.float32),
            pltpu.VMEM((nblocks, 8, rows), jnp.float32),
            dma((4,)), dma((1,)),
            dma((nblocks,)), dma((nblocks,)),
            dma((CHUNKS,)), dma((CHUNKS,)),
            dma((nblocks // 2,)), dma((1,)),
            dma((npart,)), dma((npart,)),
            dma((nblocks,)), dma((nblocks,)),
        ],
        compiler_params=pltpu.CompilerParams(
            collective_id=0, has_side_effects=True, vmem_limit_bytes=60 * 1024 * 1024
        ),
    )(snapshots.transpose(1, 0, 2), weights, offsets, freqs)
    modes, spectrum = pl.pallas_call(
        functools.partial(modes_kernel, nvars),
        out_shape=(
            jax.ShapeDtypeStruct((rows * nvars, npts), jnp.float32),
            jax.ShapeDtypeStruct((groups, nblocks), jnp.float32),
        ),
        in_specs=[vmem] * 3,
        out_specs=(vmem, vmem),
        compiler_params=pltpu.CompilerParams(vmem_limit_bytes=60 * 1024 * 1024),
    )(spectra, mixing, share)
    modes = modes.reshape(groups, nblocks, nvars, 2, npts).transpose(0, 1, 3, 2, 4)
    return modes, spectrum


def solution(mesh):
    return jax.shard_map(
        body,
        mesh=mesh,
        in_specs=(P("blk", None, "pts"), P(None, "pts"), P(), P()),
        out_specs=(P("blk", None, None, None, "pts"), P("blk", None)),
        check_vma=False,
    )
```

```python
import functools
import math

import jax
import jax.numpy as jnp
from jax import lax
from jax.experimental import pallas as pl
from jax.experimental.pallas import tpu as pltpu
from jax.sharding import PartitionSpec as P

SWEEPS = 2


HIGH = lax.Precision.HIGHEST
DAMPING = 0.01
CHUNKS = 4
MESH = pl.DeviceIdType.MESH


def half_turned(row, half):
    return pltpu.roll(row, half, 1)


def lane_gather(block, index):
    rows = max(block.shape[0], 8)
    wide = jnp.broadcast_to(block, (rows, block.shape[1]))
    index = index if index.shape == wide.shape else jnp.broadcast_to(index[:1], wide.shape)
    return jnp.take_along_axis(wide, index, axis=1, mode="promise_in_bounds")[: block.shape[0]]


def jacobi_on_lanes(gram, count, groups):
    half = groups * count
    lanes = 2 * half
    lane = lax.broadcasted_iota(jnp.int32, (8, lanes), 1)
    column = lax.rem(lane, count)
    first = lane - column
    in_real = lane[:1] < half
    row = lax.broadcasted_iota(jnp.int32, (count, lanes), 0)
    eye = jnp.where(row == column[:1], 1.0, 0.0).astype(jnp.float32)
    turned = half_turned(gram, half)
    prod_r = jnp.where(in_real, gram, turned)
    prod_i = jnp.where(in_real, turned, gram)
    diag = jnp.sum(prod_r * eye, axis=0, keepdims=True)

    def partner_of(turn):
        mirror = 2 * turn - column
        mirror = jnp.where(mirror < 0, mirror + (count - 1), mirror)
        mirror = jnp.where(mirror >= count - 1, mirror - (count - 1), mirror)
        return jnp.where(column == count - 1, turn, jnp.where(column == turn, count - 1, mirror))

    def advance(counter, carry):
        vec_r, vec_i, prod_r, prod_i, diag, partner = carry
        following = partner_of(lax.rem(counter + 1, count - 1))
        parity = jnp.where(column < partner, 1.0, -1.0).astype(jnp.float32)[:1]
        same = first + partner
        prod_sr = lane_gather(prod_r, same)
        prod_si = lane_gather(prod_i, same)
        diag_pair = lane_gather(diag, same)
        vec_sr = lane_gather(vec_r, same)
        vec_si = lane_gather(vec_i, same)
        pair_real = jnp.sum(vec_r * prod_sr + vec_i * prod_si, axis=0, keepdims=True)
        pair_imag = jnp.sum(vec_r * prod_si - vec_i * prod_sr, axis=0, keepdims=True)
        delta = parity * (diag_pair - diag)
        size4 = 4.0 * (pair_real * pair_real + pair_imag * pair_imag)
        radius = jnp.sqrt(delta * delta + size4)
        upper = radius + (delta + DAMPING * (diag + diag_pair))
        inverse = lax.rsqrt(upper * upper + size4)
        cosine = upper * inverse
        scale = 2.0 * parity * inverse
        coef_r = -scale * pair_real
        coef_i = scale * pair_imag
        sine_sq = size4 * inverse * inverse
        diag = cosine * cosine * diag + sine_sq * diag_pair - parity * cosine * size4 * inverse

        def turn_pair(real, imag, swap_real, swap_imag):
            return (
                real * cosine + (swap_real * coef_r - swap_imag * coef_i),
                imag * cosine + (swap_real * coef_i + swap_imag * coef_r),
            )

        prod_r, prod_i = turn_pair(prod_r, prod_i, prod_sr, prod_si)
        vec_r, vec_i = turn_pair(vec_r, vec_i, vec_sr, vec_si)
        return vec_r, vec_i, prod_r, prod_i, diag, following

    state = (eye, jnp.zeros_like(eye), prod_r, prod_i, diag, partner_of(0))
    state = lax.fori_loop(0, SWEEPS * (count - 1), advance, state, unroll=6)
    vec_r, vec_i, _, _, eigen, _ = state
    sum_r = jnp.sum(vec_r, axis=0, keepdims=True)
    sum_i = jnp.sum(vec_i, axis=0, keepdims=True)
    magnitude = jnp.sqrt(sum_r * sum_r + sum_i * sum_i)
    scaling = 1.0 / (jnp.maximum(magnitude, 1.0) * jnp.sqrt(count * (eigen + 1e-06)))
    phase_r = sum_r * scaling
    phase_i = -sum_i * scaling
    coef = jnp.where(
        in_real, vec_r * phase_r - vec_i * phase_i, vec_r * phase_i + vec_i * phase_r
    )
    return coef, eigen


def signed_wave(base, index):
    lanes = base.shape[1]
    value = lane_gather(base, jnp.bitwise_and(index, lanes - 1))
    return jnp.where(jnp.bitwise_and(index, lanes) == 0, value, -value)


def write_table(table_ref, offsets_ref, freqs_ref, me, groups, owners):
    rows, nfft = table_ref.shape
    half = nfft // 2
    lane = lax.broadcasted_iota(jnp.int32, (8, half), 1)
    sub = lax.broadcasted_iota(jnp.int32, (8, half), 0)
    base = jnp.cos(2.0 * math.pi / nfft * lane.astype(jnp.float32))
    own = offsets_ref[me]
    before = jnp.where(me > 0, offsets_ref[jnp.maximum(me - 1, 0)], 0)
    quarter = jnp.where(lax.rem(sub, 2) == 1, nfft // 4, 0)
    windows = {}
    for tile in range(rows // 8):
        tile_rows = range(8 * tile, 8 * tile + 8)
        pieces = tuple(r % (4 * groups) // (2 * groups) for r in tile_rows)
        freq = [owners[r // (4 * groups)] * groups + r % (2 * groups) // 2 for r in tile_rows]
        freq_rows = jnp.full((8, half), freqs_ref[freq[0]], jnp.int32)
        for s in range(2, 8, 2):
            freq_rows = jnp.where(sub >= s, freqs_ref[freq[s]], freq_rows)
        if pieces not in windows:
            tail = jnp.zeros((8, half), jnp.bool_)
            for s in range(8):
                if pieces[s]:
                    tail = tail | (sub == s)
            start = jnp.where(tail, before, own)
            window = []
            for h in range(2):
                lag = lane + h * half - start
                hann = 0.5 - 0.5 * signed_wave(base, lag)
                valid = (tail & (lag < 0)) | (jnp.logical_not(tail) & (lag >= 0))
                window.append((lag, jnp.where(valid, hann, 0.0) / math.sqrt(nfft)))
            windows[pieces] = window
        for h in range(2):
            lag, factor = windows[pieces][h]
            wave = signed_wave(base, freq_rows * lag + quarter)
            table_ref[8 * tile : 8 * tile + 8, h * half : (h + 1) * half] = factor * wave


def pipeline_kernel(
    nblocks, npart, groups, scale, energy,
    snaps_hbm, weights_hbm, offsets_hbm, freqs_hbm, spectra_hbm, mixing_ref, spectrum_ref,
    snaps_ref, weights_ref, offsets_ref, freqs_ref,
    table, stage, recv, halo, spectra, order, gram_part, total_part,
    input_sem, output_sem, send_sem, recv_sem, halo_send, halo_recv, extra_send, extra_recv,
    gram_send, gram_recv, total_send, total_recv,
):
    inputs = [
        pltpu.make_async_copy(src, dst, input_sem.at[i])
        for i, (src, dst) in enumerate((
            (offsets_hbm, offsets_ref), (freqs_hbm, freqs_ref),
            (snaps_hbm, snaps_ref), (weights_hbm, weights_ref),
        ))
    ]
    for copy in inputs:
        copy.start()
    me = lax.axis_index("blk")
    side = lax.axis_index("pts")
    nvars, nfft, npts = snaps_ref.shape
    rows = 2 * groups * nblocks
    half = rows // 2
    piece = 2 * groups
    reach = nblocks // 2
    upper_half = me // reach
    within = lax.rem(me, reach)
    far_base = (1 - upper_half) * reach
    near_base = upper_half * reach
    far = [far_base + lax.rem(within + j, reach) for j in range(reach)]
    near = [near_base + lax.rem(within + j, reach) for j in range(reach)]
    owners = far + near

    def block_peer(k):
        return lax.rem(me + k, nblocks)

    def side_peer(k):
        return lax.rem(side + k, npart)

    barrier = pltpu.get_barrier_semaphore()
    for k in range(1, nblocks):
        pl.semaphore_signal(barrier, inc=1, device_id={"blk": block_peer(k)}, device_id_type=MESH)
    for k in range(1, npart):
        pl.semaphore_signal(barrier, inc=1, device_id={"pts": side_peer(k)}, device_id_type=MESH)

    inputs[0].wait()
    inputs[1].wait()
    write_table(table, offsets_ref, freqs_ref, me, groups, owners)
    inputs[2].wait()
    snaps = jnp.concatenate([snaps_ref[v] for v in range(nvars)], axis=1)

    def transform(first):
        part = jnp.dot(
            table[2 * piece * first : 2 * piece * (first + reach), :], snaps,
            precision=lax.Precision.HIGH, preferred_element_type=jnp.float32,
        )
        for j in range(reach):
            at = 2 * piece * j
            stage[first + j, 0] = part[at : at + piece]
            stage[first + j, 1] = part[at + piece : at + 2 * piece]

    def remote(src, dst, sent, received, peer):
        return pltpu.make_async_remote_copy(
            src_ref=src, dst_ref=dst, send_sem=sent, recv_sem=received,
            device_id={"blk": peer}, device_id_type=MESH,
        )

    share = reach // CHUNKS
    before = jnp.maximum(me - 1, 0)
    after = jnp.minimum(me + 1, nblocks - 1)

    def halo_copy(chunk, peer):
        places = pl.ds(chunk * share, share)
        return remote(
            stage.at[places, 1], halo.at[places], halo_send.at[chunk], halo_recv.at[chunk], peer
        )

    def far_copy(j, slot, peer):
        return remote(stage.at[j, 0], recv.at[slot, 0], send_sem.at[j], recv_sem.at[slot], peer)

    def near_copy(j, slot, peer):
        at = reach + j
        return remote(stage.at[at], recv.at[slot], send_sem.at[at], recv_sem.at[slot], peer)

    def extra_copy(j):
        return remote(stage.at[j, 1], recv.at[reach, 1], extra_send.at[j], extra_recv.at[0], far[j])

    transform(0)
    pl.semaphore_wait(barrier, nblocks - 1 + npart - 1)

    @pl.when(within != 0)
    def _():
        for chunk in range(CHUNKS):
            halo_copy(chunk, before).start()

    @pl.when(me == reach)
    def _():
        for j in range(reach):
            extra_copy(j).start()

    transform(reach)
    for j in range(1, share + 1):
        near_copy(j, me, near[j]).start()
    for chunk in range(CHUNKS):
        places = [(chunk * share + i, (chunk * share + i + 1) % reach) for i in range(share)]

        @pl.when(within != reach - 1)
        def _():
            halo_copy(chunk, after).wait_recv()
            for theirs, mine in places:
                stage[mine, 0] = stage[mine, 0] + halo[theirs]

        for _, mine in places:
            far_copy(mine, me, far[mine]).start()
    for j in range(share + 1, reach):
        near_copy(j, me, near[j]).start()

    recv[me] = stage[reach]
    empty = jnp.zeros(recv.shape[2:], jnp.float32)
    recv[nblocks, 1] = empty
    for i in range(1, reach):
        recv[far_base + i, 1] = empty

    @pl.when(upper_half == 1)
    def _():
        recv[0, 1] = empty

    @pl.when(upper_half == 0)
    def _():
        extra_copy(0).wait_recv()

    for j in range(reach):
        far_copy(j, far[j], far[j]).wait_recv()
    for j in range(1, reach):
        near_copy(j, near[j], near[j]).wait_recv()
    inputs[3].wait()

    combined = recv[0:nblocks, 0] + recv[1 : nblocks + 1, 1]
    spectra[...] = combined.reshape(rows, nvars * npts)
    spectra_out = pltpu.make_async_copy(spectra, spectra_hbm, output_sem.at[0])
    spectra_out.start()

    weight = jnp.concatenate([weights_ref[v : v + 1, :] for v in range(nvars)], axis=1)
    gram_all = lax.dot_general(
        spectra[...] * weight, spectra[...], (((1,), (1,)), ((), ())),
        precision=HIGH, preferred_element_type=jnp.float32,
    )
    lane = lax.broadcasted_iota(jnp.int32, (1, rows), 1)
    sign = jnp.where(lane < half, 1.0, -1.0).astype(jnp.float32)
    group_of = lax.rem(lane, half) // nblocks
    arrival = lax.rem(lane, nblocks) * piece + 2 * group_of + jnp.where(lane < half, 0, 1)
    order[...] = lane_gather(gram_all, arrival).reshape(order.shape)
    gram = jnp.zeros((nblocks, rows), jnp.float32)
    for f in range(groups):
        upper = order[:, 2 * f, :]
        lower = order[:, 2 * f + 1, :]
        gram = jnp.where(group_of == f, upper + sign * pltpu.roll(lower, half, 1), gram)
    gram_part[side] = gram * scale

    def gram_copy(k, slot):
        peer = side_peer(k)
        return pltpu.make_async_remote_copy(
            src_ref=gram_part.at[side], dst_ref=gram_part.at[slot], send_sem=gram_send.at[k],
            recv_sem=gram_recv.at[slot], device_id={"pts": peer}, device_id_type=MESH,
        )

    for k in range(1, npart):
        gram_copy(k, side).start()
    for k in range(1, npart):
        gram_copy(k, side_peer(k)).wait_recv()
    gram = gram_part[0]
    for k in range(1, npart):
        gram = gram + gram_part[k]

    row = lax.broadcasted_iota(jnp.int32, (nblocks, rows), 0)
    trace = jnp.where((row == lax.rem(lane, nblocks)) & (lane < half), gram, 0.0)
    trace = jnp.sum(jnp.sum(trace, axis=0, keepdims=True), axis=1, keepdims=True)
    total_part[me] = jnp.broadcast_to(trace, total_part.shape[1:])

    def total_copy(k, slot):
        peer = block_peer(k)
        return pltpu.make_async_remote_copy(
            src_ref=total_part.at[me], dst_ref=total_part.at[slot], send_sem=total_send.at[k],
            recv_sem=total_recv.at[slot], device_id={"blk": peer}, device_id_type=MESH,
        )

    for k in range(1, nblocks):
        total_copy(k, me).start()

    coef, eigen = jacobi_on_lanes(gram, nblocks, groups)

    turned = -sign * half_turned(coef, half)
    for ri, block in enumerate((coef, turned)):
        for f in range(groups):
            order[:, 2 * f + ri, :] = jnp.where(group_of == f, block, 0.0)
    mixing_ref[...] = order[...].reshape(rows, rows).T

    for k in range(1, nblocks):
        total_copy(k, block_peer(k)).wait_recv()
    total = jnp.sum(total_part[...], axis=0)
    share_of = energy * eigen / total[:1]
    for f in range(groups):
        spectrum_ref[f : f + 1, :] = share_of[:, f * nblocks : (f + 1) * nblocks]
    spectra_out.wait()
    for j in range(reach):
        far_copy(j, me, far[j]).wait_send()
    for j in range(1, reach):
        near_copy(j, me, near[j]).wait_send()

    @pl.when(within != 0)
    def _():
        for chunk in range(CHUNKS):
            halo_copy(chunk, before).wait_send()

    @pl.when(me == reach)
    def _():
        for j in range(reach):
            extra_copy(j).wait_send()

    for k in range(1, nblocks):
        total_copy(k, me).wait_send()
    for k in range(1, npart):
        gram_copy(k, side).wait_send()


def modes_kernel(nvars, spectra_ref, mixing_ref, share_ref, modes_ref, spectrum_ref):
    rows, width = spectra_ref.shape
    half = rows // 2
    npts = width // nvars
    spectrum_ref[...] = share_ref[...]
    modes = jnp.dot(
        mixing_ref[...], spectra_ref[...], precision=lax.Precision.HIGH,
        preferred_element_type=jnp.float32,
    )
    for v in range(nvars):
        for ri in range(2):
            modes_ref[pl.ds(2 * v + ri, half, stride=2 * nvars), :] = modes[
                ri * half : (ri + 1) * half, v * npts : (v + 1) * npts
            ]


def body(snapshots, weights, offsets, freqs):
    nfft, nvars, npts = snapshots.shape
    nfreq = freqs.shape[0]
    nblocks = lax.axis_size("blk")
    npart = lax.axis_size("pts")
    groups = nfreq // nblocks
    width = nvars * npts
    rows = 2 * nfreq
    scale = 1.0 / (nblocks * nvars * npts * npart)
    dma = pltpu.SemaphoreType.DMA
    vmem = pl.BlockSpec(memory_space=pltpu.VMEM)
    far_memory = pl.BlockSpec(memory_space=pltpu.HBM)
    spectra, mixing, share = pl.pallas_call(
        functools.partial(pipeline_kernel, nblocks, npart, groups, scale, float(nfreq * nblocks)),
        out_shape=(
            jax.ShapeDtypeStruct((rows, width), jnp.float32),
            jax.ShapeDtypeStruct((rows, rows), jnp.float32),
            jax.ShapeDtypeStruct((groups, nblocks), jnp.float32),
        ),
        in_specs=[far_memory] * 4,
        out_specs=(far_memory, vmem, vmem),
        scratch_shapes=[
            pltpu.VMEM((nvars, nfft, npts), jnp.float32),
            pltpu.VMEM((nvars, npts), jnp.float32),
            pltpu.SMEM((nblocks,), jnp.int32),
            pltpu.SMEM((nfreq,), jnp.int32),
            pltpu.VMEM((2 * rows, nfft), jnp.float32),
            pltpu.VMEM((nblocks, 2, 2 * groups, width), jnp.float32),
            pltpu.VMEM((nblocks + 1, 2, 2 * groups, width), jnp.float32),
            pltpu.VMEM((nblocks // 2, 2 * groups, width), jnp.float32),
            pltpu.VMEM((rows, width), jnp.float32),
            pltpu.VMEM((nblocks, 2 * groups, rows), jnp.float32),
            pltpu.VMEM((npart, nblocks, rows), jnp.float32),
            pltpu.VMEM((nblocks, 8, rows), jnp.float32),
            dma((4,)), dma((1,)),
            dma((nblocks,)), dma((nblocks,)),
            dma((CHUNKS,)), dma((CHUNKS,)),
            dma((nblocks // 2,)), dma((1,)),
            dma((npart,)), dma((npart,)),
            dma((nblocks,)), dma((nblocks,)),
        ],
        compiler_params=pltpu.CompilerParams(
            collective_id=0, has_side_effects=True, vmem_limit_bytes=60 * 1024 * 1024
        ),
    )(snapshots.transpose(1, 0, 2), weights, offsets, freqs)
    modes, spectrum = pl.pallas_call(
        functools.partial(modes_kernel, nvars),
        out_shape=(
            jax.ShapeDtypeStruct((rows * nvars, npts), jnp.float32),
            jax.ShapeDtypeStruct((groups, nblocks), jnp.float32),
        ),
        in_specs=[vmem] * 3,
        out_specs=(vmem, vmem),
        compiler_params=pltpu.CompilerParams(vmem_limit_bytes=60 * 1024 * 1024),
    )(spectra, mixing, share)
    modes = modes.reshape(groups, nblocks, nvars, 2, npts).transpose(0, 1, 3, 2, 4)
    return modes, spectrum


def solution(mesh):
    return jax.shard_map(
        body,
        mesh=mesh,
        in_specs=(P("blk", None, "pts"), P(None, "pts"), P(), P()),
        out_specs=(P("blk", None, None, None, "pts"), P("blk", None)),
        check_vma=False,
    )
```
